512 devices in a mesh: scan: 32 (over z, core), depth: 16 (over y, x).
Axes of the slice: x: 4, y: 4, z: 16, core: 2. Of those that a mesh axis runs over, the one named last changes fastest.
Arguments:
- object_slices: float32 [16, 2, 8192, 128], P('depth', None, 'scan'), may hold values from -4 to 4
- probe_wave: float32 [2, 128, 128], replicated, may hold values from -6 to 6
- intensities: float32 [64, 128, 128], P('scan'), may hold values from 0.1 to 4
- offsets: int32 [64], P('scan'), may hold values from 0 to 255, as said below
- owners: int32 [64], P('scan'), may hold values from 0 to 31, as said below
Outputs:
- object_next: float32 [16, 2, 8192, 128], P('depth', None, 'scan')
The draws below stay inside these ranges and needn't reach their ends.
Inputs may be any that keep to these rules, and one draw needn't show every extreme that they name: Position p is held by scan index p // 2; its window ends at row owners[p] * 256 + offsets[p] + 127, which is below 8192. owners[p] is p // 2 or one less.
All inputs are finite; a program needn't handle non-finite values.
Results may differ from the reference program's by a relative error of at most 0.0003.
Values sent between devices are 32-bit elements; how exact they have to be, the bound alone decides.
No kernel may reach another device: no remote copies, remote signals or barrier semaphores. Data moves between devices by JAX's collectives and lax.ppermute only.
A program may use at most 64 MiB of HBM per device.

```python
import math
import jax
import jax.numpy as jnp
from jax import lax

WIN = 128
TR = 256
POS_DEV = 2
SLICES = 16
ROWS = 8192
POSITIONS = 64


def position_draw(key):
    owner_key, offset_key = jax.random.split(key)
    position = jnp.arange(POSITIONS, dtype=jnp.int32)
    holder = position // POS_DEV
    step_back = jax.random.randint(owner_key, (POSITIONS,), 0, 2, dtype=jnp.int32)
    step_back = jnp.where((holder == 0) | (position == POS_DEV) | (position == POSITIONS - POS_DEV), 0, step_back)
    step_back = jnp.where(position == POSITIONS - 1, 1, step_back)
    owner_tile = holder - step_back
    offset_rows = jax.random.randint(offset_key, (POSITIONS,), 0, TR, dtype=jnp.int32)
    offset_rows = jnp.minimum(offset_rows, ROWS - WIN - owner_tile * TR)
    offset_rows = jnp.where(position == 0, 0, offset_rows)
    offset_rows = jnp.where(position == POS_DEV, TR - 1, offset_rows)
    return (owner_tile.astype(jnp.int32), offset_rows.astype(jnp.int32))


def draw_offsets(key, part):
    owner_tile, offset_rows = position_draw(key)
    return offset_rows


def draw_owners(key, part):
    owner_tile, offset_rows = position_draw(key)
    return owner_tile


def shard_levels(key, extent, cuts, least, high):
    def one(axis_at, shards_of):
        steps = jax.random.uniform(jax.random.fold_in(jax.random.fold_in(key, 6), axis_at), (shards_of,), jnp.float32, least / len(cuts), high / len(cuts))
        return jnp.repeat(jnp.exp(steps), extent[axis_at] // shards_of).reshape((-1,) + (1,) * (len(extent) - axis_at - 1))

    level = one(*cuts[0])
    for cut in cuts[1:]:
        level = level * one(*cut)
    return level


def noise(stream_key, dims, width, bound, cuts=(), kind=jnp.bfloat16):
    values = width * jax.random.normal(stream_key, dims, jnp.float32)
    if cuts:
        values = values * shard_levels(stream_key, dims, cuts, -0.22, 0.18)
    return jnp.clip(values, -bound, bound).astype(kind)


def setup_inputs(seed: int = 0) -> dict:
    arg_keys = jax.random.split(jax.random.key(seed), 6)
    return {
        "object_slices": noise(arg_keys[0], (SLICES, 2, ROWS, WIN), 0.7071, 4.0, ((0, 16), (2, 32)), jnp.float32),
        "probe_wave": noise(arg_keys[1], (2, WIN, WIN), 1.0, 6.0, (), jnp.float32),
        "intensities": jnp.clip(jnp.exp(math.log(4.0) - 3.6888794 * jax.random.uniform(arg_keys[2], (POSITIONS, WIN, WIN), jnp.float32) ** shard_levels(arg_keys[2], (POSITIONS, WIN, WIN), ((0, 32),), -0.2, 0.2)), 0.1, 4.0),
        "offsets": draw_offsets(jax.random.fold_in(arg_keys[5], 71), 0),
        "owners": draw_owners(jax.random.fold_in(arg_keys[5], 71), 0),
    }


exact_mode = lax.Precision.HIGHEST
step_size = 0.25

def tables(win_size):
    indices = jnp.arange(win_size, dtype=jnp.int32)
    product = indices[:, None] * indices[None, :] % win_size
    angles = product.astype(jnp.float32) * (2.0 * math.pi / win_size)
    norm_scale = 1.0 / math.sqrt(win_size)
    cos_table = jnp.cos(angles) * norm_scale
    sin_table = jnp.sin(angles) * norm_scale
    frequency = jnp.where(indices < win_size // 2, indices, indices - win_size).astype(jnp.float32)
    phases = -(math.pi / win_size) * (frequency[:, None] * frequency[:, None] + frequency[None, :] * frequency[None, :])
    forward_table = jnp.stack([jnp.stack([cos_table, sin_table]), jnp.stack([-sin_table, cos_table])])
    backward_table = jnp.stack([jnp.stack([cos_table, -sin_table]), jnp.stack([sin_table, cos_table])])
    return (forward_table, backward_table, jnp.cos(phases), jnp.sin(phases))

def transform(stacked, table):
    left_done = jnp.einsum('abkn,...bnm->...akm', table, stacked, precision=exact_mode)
    return jnp.einsum('...bkn,abnm->...akm', left_done, table, precision=exact_mode)

def propagate(stacked, tables_set, conj_sign):
    spec = transform(stacked, tables_set[0])
    kernel_cos, kernel_sin = (tables_set[2], tables_set[3])
    spec_real, spec_imag = (spec[..., 0, :, :], spec[..., 1, :, :])
    phased_real = spec_real * kernel_cos - conj_sign * spec_imag * kernel_sin
    phased_imag = spec_imag * kernel_cos + conj_sign * spec_real * kernel_sin
    return transform(jnp.stack([phased_real, phased_imag], -3), tables_set[1])

def mix_wave(wave_now, window):
    mixed_real = wave_now[..., 0, :, :] * window[..., 0, :, :] - wave_now[..., 1, :, :] * window[..., 1, :, :]
    mixed_imag = wave_now[..., 0, :, :] * window[..., 1, :, :] + wave_now[..., 1, :, :] * window[..., 0, :, :]
    return jnp.stack([mixed_real, mixed_imag], -3)

def advance(wave_now, window, tables_set):
    return propagate(mix_wave(wave_now, window), tables_set, 1.0)

def retreat(adjoint, window, tables_set):
    back_real = window[..., 0, :, :] * adjoint[..., 0, :, :] + window[..., 1, :, :] * adjoint[..., 1, :, :]
    back_imag = window[..., 0, :, :] * adjoint[..., 1, :, :] - window[..., 1, :, :] * adjoint[..., 0, :, :]
    return propagate(jnp.stack([back_real, back_imag], -3), tables_set, -1.0)

def far_field(wave_now, window, measured, tables_set):
    far_wave = transform(mix_wave(wave_now, window), tables_set[0])
    far_real, far_imag = (far_wave[..., 0, :, :], far_wave[..., 1, :, :])
    residual = far_real * far_real + far_imag * far_imag - measured
    return transform(jnp.stack([residual * far_real, residual * far_imag], -3), tables_set[1])

def object_grad(wave_now, adjoint):
    grad_real = wave_now[..., 0, :, :] * adjoint[..., 0, :, :] + wave_now[..., 1, :, :] * adjoint[..., 1, :, :]
    grad_imag = wave_now[..., 0, :, :] * adjoint[..., 1, :, :] - wave_now[..., 1, :, :] * adjoint[..., 0, :, :]
    return jnp.stack([grad_real, grad_imag], -3)

def reference(object_slices, probe_wave, intensities, offsets, owners):
    win_size = probe_wave.shape[-1]
    tables_set = tables(win_size)
    row_starts = (owners * TR + offsets).astype(jnp.int32)
    layers = object_slices.shape[0]

    def accumulate(gradient, inputs):
        row_begin, measured = inputs
        row_begin = row_begin.astype(jnp.int32)
        windows = lax.dynamic_slice_in_dim(object_slices, row_begin, win_size, 2)
        wave_now = probe_wave
        entering = []
        for layer_index in range(layers):
            entering.append(wave_now)
            if layer_index < layers - 1:
                wave_now = advance(wave_now, windows[layer_index], tables_set)
        adjoint = far_field(wave_now, windows[layers - 1], measured, tables_set)
        pieces = [None] * layers
        for layer_index in range(layers - 1, -1, -1):
            pieces[layer_index] = object_grad(entering[layer_index], adjoint)
            if layer_index > 0:
                adjoint = retreat(adjoint, windows[layer_index], tables_set)
        update = jnp.stack(pieces)
        current = lax.dynamic_slice_in_dim(gradient, row_begin, win_size, 2)
        gradient = lax.dynamic_update_slice_in_dim(gradient, current + update, row_begin, 2)
        return (gradient, None)
    gradient, unused_out = lax.scan(accumulate, jnp.zeros_like(object_slices), (row_starts, intensities))
    return object_slices - step_size * gradient
```

```python
import functools

import jax
import jax.numpy as jnp
import ml_dtypes
import numpy as np
from jax import lax
from jax.experimental import pallas as pl
from jax.experimental.pallas import tpu as pltpu
from jax.sharding import PartitionSpec as P

step_size = 0.25
side = 128
tile = 256
slab_rows = 2 * tile + side
group = 8
swap = 5
params = pltpu.CompilerParams(vmem_limit_bytes=48 * 2**20)
in_vmem = pl.BlockSpec(memory_space=pltpu.VMEM)
in_smem = pl.BlockSpec(memory_space=pltpu.SMEM)
window_type = jax.ShapeDtypeStruct((2, side, side), jnp.float32)
stack_type = jax.ShapeDtypeStruct((group, 2, side, side), jnp.float32)


def two_parts(table):
    table = table.astype(np.float32)
    high = table.astype(ml_dtypes.bfloat16)
    low = (table - high.astype(np.float32)).astype(ml_dtypes.bfloat16)
    return high, low


def both_sides(matrix):
    left = np.block([[matrix.real, -matrix.imag], [matrix.imag, matrix.real]])
    right = np.block([[matrix.real, matrix.imag], [-matrix.imag, matrix.real]])
    return two_parts(left) + two_parts(right)


def tables():
    index = np.arange(side)
    angles = 2.0 * np.pi * (index[:, None] * index[None, :] % side) / side
    fourier = (np.cos(angles) - 1j * np.sin(angles)) / np.sqrt(side)
    frequency = np.where(index < side // 2, index, index - side).astype(np.float64)
    phase = np.exp(-1j * np.pi / side * frequency * frequency)
    step = np.conj(fourier) @ (phase[:, None] * fourier)
    return both_sides(step), both_sides(fourier)


def split(x):
    high = x.astype(jnp.bfloat16)
    return high, (x - high.astype(jnp.float32)).astype(jnp.bfloat16)


def dot(a, b):
    return jnp.dot(a, b, preferred_element_type=jnp.float32)


def two_sided(real, imag, table):
    left_high, left_low, right_high, right_low = table
    high, low = split(jnp.concatenate([real, imag], 0))
    both = dot(left_high[...], jnp.concatenate([high, low], 1))
    left = both[:, :side] + both[:, side:] + dot(left_low[...], high)
    high, low = split(jnp.concatenate([left[:side], left[side:]], 1))
    done = dot(high, right_high[...]) + (dot(low, right_high[...]) + dot(high, right_low[...]))
    return done[:, :side], done[:, side:]


def times(a, b):
    return a[0] * b[0] - a[1] * b[1], a[0] * b[1] + a[1] * b[0]


def pair(ref, *at):
    return ref[(*at, 0)], ref[(*at, 1)]


def put(ref, value, *at):
    ref[(*at, 0)] = value[0]
    ref[(*at, 1)] = value[1]


def cut_kernel(starts, low, block, high, odd_out, even_out, slab):
    slab[:, :tile] = low[...]
    slab[:, tile : 2 * tile] = block[...]
    slab[:, 2 * tile :] = high[...]
    for at, out in ((0, odd_out), (1, even_out)):
        out[...] = slab[:, pl.ds(starts[at], side), :]


def upper_kernel(*refs):
    probe, arrived, table = refs[0], refs[1 : 1 + group], refs[1 + group : 5 + group]
    wave_out, waves, windows = refs[5 + group :]
    me = lax.axis_index("depth") & (group - 1)
    for turn in range(group):
        windows[turn ^ me] = arrived[turn][...]
    wave = pair(probe)
    for layer in range(group):
        put(waves, wave, layer)
        wave = two_sided(*times(wave, pair(windows, layer)), table)
    put(wave_out, wave)


def middle_kernel(*refs):
    entering, windows, late, measured = refs[:4]
    table, fourier = refs[4:8], refs[8:12]
    adjoint_out, parts = refs[12], refs[13 : 13 + group]
    held, waves, updates = refs[13 + group :]
    depth = lax.axis_index("depth")
    me = depth & (group - 1)
    first = 2 * (1 - (lax.axis_index("scan") & 1))
    which = jnp.where((me ^ first) == 0, 0, 1)
    held[...] = windows[...]
    held[me] = late[...]
    wave = pair(entering)
    for layer in range(group):
        put(waves, wave, layer)
        last = layer == group - 1
        wave = two_sided(*times(wave, pair(held, layer)), fourier if last else table)
    far_real, far_imag = wave
    residual = far_real * far_real + far_imag * far_imag - measured[which]
    adjoint = two_sided(residual * far_real, -(residual * far_imag), fourier)
    for layer in reversed(range(group)):
        real, imag = times(pair(waves, layer), adjoint)
        put(updates, (real, -imag), layer)
        adjoint = two_sided(*times(pair(held, layer), adjoint), table)
    put(adjoint_out, adjoint)
    for turn in range(group):
        parts[turn][...] = updates[turn ^ me]


def lower_kernel(*refs):
    returned, waves, windows = refs[:3]
    theirs, table = refs[3 : 3 + group], refs[3 + group : 7 + group]
    parts, updates = refs[7 + group : 7 + 2 * group], refs[-1]
    depth = lax.axis_index("depth")
    me = depth & (group - 1)
    mine = (me ^ (2 * (lax.axis_index("scan") & 1)))
    is_upper = (mine == 0) | (mine == swap)
    adjoint = pair(returned)
    for layer in reversed(range(group)):
        real, imag = times(pair(waves, layer), adjoint)
        put(updates, (real, -imag), layer)
        if layer:
            adjoint = two_sided(*times(pair(windows, layer), adjoint), table)

    @pl.when(is_upper)
    def _():
        for turn in range(group):
            parts[turn][...] = updates[turn ^ me]

    @pl.when(jnp.logical_not(is_upper))
    def _():
        for turn in range(group):
            parts[turn][...] = theirs[turn][...]


def place_kernel(*refs):
    starts, own, arrived = refs[0], refs[1], refs[2 : 2 + group]
    up, middle, down, slab = refs[2 + group :]
    depth = lax.axis_index("depth")
    mine = depth ^ (2 * (lax.axis_index("scan") & 1))
    is_upper = (mine == 0) | (mine == swap)
    slab[...] = jnp.zeros_like(slab)
    odd = (arrived[1][...] + arrived[3][...]) + (arrived[5][...] + arrived[7][...])
    even = (arrived[2][...] + arrived[4][...]) + arrived[6][...]
    even = even + jnp.where(is_upper, own[...], arrived[0][...])
    for at, update in ((0, odd), (1, even)):
        rows = pl.ds(starts[at], side)
        slab[:, rows, :] = slab[:, rows, :] + update
    up[...] = slab[:, :tile]
    middle[...] = slab[:, tile : 2 * tile]
    down[...] = slab[:, 2 * tile :]


def last_kernel(block, middle, below, above, out):
    head = middle[:, :side] + below[:, :side] + above[...]
    tail = middle[:, side:] + below[:, side:]
    out[0, :, :side] = block[:, :side] - step_size * head
    out[0, :, side:] = block[:, side:] - step_size * tail


def shards(object_slices, probe_wave, intensities, offsets, owners):
    scans = lax.axis_size("scan")
    depths = lax.axis_size("depth")
    scan_index = lax.axis_index("scan")
    depth_index = lax.axis_index("depth")
    axes = ("scan", "depth")
    step_tables, fourier_tables = tables()
    vmem = functools.partial(pl.pallas_call, compiler_params=params)

    def at(scan, depth):
        return scan * depths + depth

    targets = [(i, (2 * (i & 1)) ^ (swap * q)) for i in range(scans) for q in range(2)]
    gathers = []
    for turn in range(group):
        pairs = []
        for i, target in targets:
            if turn:
                pairs.append((at(i, target ^ turn), at(i, target)))
            pairs.append((at(i, group + (target ^ turn)), at(i ^ 1, target)))
        gathers.append(pairs)
    scatters = [[(b, a) for a, b in pairs] for pairs in gathers]
    across = [(at(i, target), at(i ^ 1, target)) for i, target in targets]
    back = [(b, a) for a, b in across]
    onward = [(i, i + 1) for i in range(scans - 1)]
    rearward = [(i + 1, i) for i in range(scans - 1)]

    block = object_slices[0]
    low = lax.ppermute(block, "scan", onward)
    high = lax.ppermute(block[:, :side], "scan", rearward)
    measured = lax.ppermute(intensities, axes, across)

    starts = jnp.clip((owners - scan_index + 1) * tile + offsets, 0, 2 * tile)
    is_odd = ((depth_index ^ (2 * (scan_index & 1))) & 1) == 1
    starts = jnp.where(is_odd, starts, starts[::-1])
    odd_window, even_window = vmem(
        cut_kernel,
        out_shape=[window_type] * 2,
        in_specs=[in_smem] + [in_vmem] * 3,
        out_specs=[in_vmem] * 2,
        scratch_shapes=[pltpu.VMEM((2, slab_rows, side), jnp.float32)],
        name="cut",
    )(starts, low, block, high)

    arrived = [even_window]
    for turn in range(1, group):
        arrived.append(
            lax.ppermute(odd_window if turn & 1 else even_window, axes, gathers[turn])
        )
    wave, waves, windows = vmem(
        upper_kernel,
        out_shape=[window_type, stack_type, stack_type],
        in_specs=[in_vmem] * (5 + group),
        out_specs=[in_vmem] * 3,
        name="upper",
    )(probe_wave, *arrived, *step_tables)
    entering = lax.ppermute(wave, axes, across)
    late = lax.ppermute(even_window, axes, gathers[0])

    adjoint, *lower_parts = vmem(
        middle_kernel,
        out_shape=[window_type] * (1 + group),
        in_specs=[in_vmem] * 12,
        out_specs=[in_vmem] * (1 + group),
        scratch_shapes=[pltpu.VMEM(stack_type.shape, jnp.float32)] * 3,
        name="middle",
    )(entering, windows, late, measured, *step_tables, *fourier_tables)
    returned = lax.ppermute(adjoint, axes, back)
    first_back = lax.ppermute(lower_parts[0], axes, scatters[0])

    parts = vmem(
        lower_kernel,
        out_shape=[window_type] * group,
        in_specs=[in_vmem] * (7 + group),
        out_specs=[in_vmem] * group,
        scratch_shapes=[pltpu.VMEM(stack_type.shape, jnp.float32)],
        name="lower",
    )(returned, waves, windows, *lower_parts, *step_tables)
    landed = [first_back] + [
        lax.ppermute(parts[turn], axes, scatters[turn]) for turn in range(1, group)
    ]

    up, middle, down = vmem(
        place_kernel,
        out_shape=[
            jax.ShapeDtypeStruct((2, tile, side), jnp.float32),
            jax.ShapeDtypeStruct((2, tile, side), jnp.float32),
            jax.ShapeDtypeStruct((2, side, side), jnp.float32),
        ],
        in_specs=[in_smem] + [in_vmem] * (1 + group),
        out_specs=[in_vmem] * 3,
        scratch_shapes=[pltpu.VMEM((2, slab_rows, side), jnp.float32)],
        name="place",
    )(starts, parts[0], *landed)
    below = lax.ppermute(up, "scan", rearward)
    above = lax.ppermute(down, "scan", onward)
    return vmem(
        last_kernel,
        out_shape=jax.ShapeDtypeStruct(object_slices.shape, jnp.float32),
        in_specs=[in_vmem] * 4,
        out_specs=in_vmem,
        name="last",
    )(block, middle, below, above)


def solution(mesh):
    return jax.shard_map(
        shards,
        mesh=mesh,
        in_specs=(P("depth", None, "scan", None), P(), P("scan", None, None), P("scan"), P("scan")),
        out_specs=P("depth", None, "scan", None),
        check_vma=False,
    )
```

```python
import functools

import jax
import jax.numpy as jnp
import numpy as np
from jax import lax
from jax.experimental import pallas as pl
from jax.experimental.pallas import tpu as pltpu
from jax.sharding import PartitionSpec as P

step_size = 0.25
side = 128
tile = 256
group = 8
half = group // 2
rounds = ((0, 1, 2, 3, 4, 5, 6, 7), (0, 7, 6, 5, 4, 1, 2, 3))
first_target = (0, 6)
params = pltpu.CompilerParams(vmem_limit_bytes=48 * 2**20)
in_vmem = pl.BlockSpec(memory_space=pltpu.VMEM)
in_smem = pl.BlockSpec(memory_space=pltpu.SMEM)
window_type = jax.ShapeDtypeStruct((2, side, side), jnp.float32)
tile_type = jax.ShapeDtypeStruct((2, tile, side), jnp.float32)
stack_type = jax.ShapeDtypeStruct((half, 2, side, side), jnp.float32)


def tables():
    index = np.arange(side)
    angles = 2.0 * np.pi * (index[:, None] * index[None, :] % side) / side
    fourier = (np.cos(angles) - 1j * np.sin(angles)) / np.sqrt(side)
    frequency = np.where(index < side // 2, index, index - side).astype(np.float64)
    phase = np.exp(-1j * np.pi / side * frequency * frequency)
    step = np.conj(fourier) @ (phase[:, None] * fourier)
    return [np.stack([m.real, m.imag]).astype(np.float32) for m in (step, fourier)]


def split(x):
    high = x.astype(jnp.bfloat16)
    return high, (x - high.astype(jnp.float32)).astype(jnp.bfloat16)


def dot(a, b):
    return jnp.dot(a, b, preferred_element_type=jnp.float32)


def beside(*parts):
    return jnp.concatenate(parts, 1)


def above(*parts):
    return jnp.concatenate(parts, 0)


def blocks(ref):
    real, imag = split(ref[0]), split(ref[1])
    left = [above(beside(r, -i), beside(i, r)) for r, i in zip(real, imag)]
    right = [above(beside(r, i), beside(-i, r)) for r, i in zip(real, imag)]
    return left, right


def two_sided(wave, table):
    (left_high, left_low), (right_high, right_low) = table
    high, low = split(above(*wave))
    both = dot(left_high, beside(high, low))
    left = both[:, :side] + both[:, side:] + dot(left_low, high)
    high, low = split(beside(left[:side], left[side:]))
    done = dot(high, right_high) + (dot(low, right_high) + dot(high, right_low))
    return done[:, :side], done[:, side:]


def times(a, b):
    return a[0] * b[0] - a[1] * b[1], a[0] * b[1] + a[1] * b[0]


def pair(ref, *at):
    return ref[(*at, 0)], ref[(*at, 1)]


def put(ref, value, *at):
    ref[(*at, 0)] = value[0]
    ref[(*at, 1)] = value[1]


def place_in_group():
    me = lax.axis_index("depth") & (group - 1)
    return me, me >= half


def slot(me, kind, turn):
    return me ^ jnp.where(kind, rounds[1][turn], rounds[0][turn])


def is_upper():
    mine = lax.axis_index("depth") - first_target[1] * (lax.axis_index("scan") & 1)
    return (mine == 0) | (mine == 1)


def start_of(at, owners, offsets):
    start = (owners[at] - lax.axis_index("scan") + 1) * tile + offsets[at]
    return jnp.clip(start, 0, 2 * tile)


def cut_kernel(owners, offsets, block, near, far, odd_out, even_out, slab):
    slab[:, tile : 2 * tile] = block[...]
    even_scan = (lax.axis_index("scan") & 1) == 0

    @pl.when(even_scan)
    def _():
        slab[:, :tile] = far[...]
        slab[:, 2 * tile :] = near[...]

    @pl.when(jnp.logical_not(even_scan))
    def _():
        slab[:, :tile] = near[...]
        slab[:, 2 * tile :] = far[...]

    odd_position = 1 - (lax.axis_index("depth") & 1)
    for at, out in ((odd_position, odd_out), (1 - odd_position, even_out)):
        out[...] = slab[:, pl.ds(start_of(at, owners, offsets), side), :]


def forward(wave, windows, waves, table):
    for layer in range(half):
        put(waves, wave, layer)
        wave = two_sided(times(wave, pair(windows, layer)), table)
    return wave


def upper_kernel(probe, own, late, one, two, three, four, table_ref, wave_out, waves, windows):
    me, kind = place_in_group()
    arrived = (None, one, two, three)
    for turn in (1, 2, 3):
        windows[slot(me, kind, turn)] = arrived[turn][...]

    @pl.when(kind)
    def _():
        windows[me ^ rounds[1][4]] = four[...]

    @pl.when(jnp.logical_not(kind) & is_upper())
    def _():
        windows[me & (half - 1)] = own[...]

    @pl.when(jnp.logical_not(kind) & jnp.logical_not(is_upper()))
    def _():
        windows[me & (half - 1)] = late[...]

    put(wave_out, forward(pair(probe), windows, waves, blocks(table_ref)))


def second_kernel(wave_in, own, late, four, five, six, seven, table_ref, wave_out, waves, windows):
    me, kind = place_in_group()
    arrived = (five, six, seven)
    for turn in (5, 6, 7):
        windows[slot(me, kind, turn) & (half - 1)] = arrived[turn - 5][...]

    @pl.when(jnp.logical_not(kind))
    def _():
        windows[(me ^ rounds[0][4]) & (half - 1)] = four[...]

    @pl.when(kind & is_upper())
    def _():
        windows[me & (half - 1)] = own[...]

    @pl.when(kind & jnp.logical_not(is_upper()))
    def _():
        windows[me & (half - 1)] = late[...]

    put(wave_out, forward(pair(wave_in), windows, waves, blocks(table_ref)))


def backward(adjoint, windows, waves, updates, base, table, last):
    for layer in reversed(range(half)):
        real, imag = times(pair(waves, layer), adjoint)
        put(updates, (real, -imag), base + layer)
        if layer or not last:
            adjoint = two_sided(times(pair(windows, layer), adjoint), table)
    return adjoint


def middle_kernel(entering, front, rear, measured, table_ref, fourier_ref, adjoint_out, *rest):
    parts, (waves, updates) = rest[:group], rest[group:]
    me, kind = place_in_group()
    table, fourier = blocks(table_ref), blocks(fourier_ref)
    wave = pair(entering)
    for layer in range(group):
        put(waves, wave, layer)
        window = pair(front if layer < half else rear, layer % half)
        wave = two_sided(times(wave, window), fourier if layer == group - 1 else table)
    far_real, far_imag = wave
    residual = far_real * far_real + far_imag * far_imag - measured[me & 1]
    adjoint = two_sided((residual * far_real, -(residual * far_imag)), fourier)
    for layer in reversed(range(group)):
        real, imag = times(pair(waves, layer), adjoint)
        put(updates, (real, -imag), layer)
        window = pair(front if layer < half else rear, layer % half)
        adjoint = two_sided(times(window, adjoint), table)
    put(adjoint_out, adjoint)
    for turn in range(group):
        parts[turn][...] = updates[slot(me, kind, turn)]


def lower_kernel(returned, front, front_waves, rear, rear_waves, table_ref, *rest):
    theirs, parts, updates = rest[:group], rest[group : 2 * group], rest[-1]
    me, kind = place_in_group()
    upper = is_upper()
    table = blocks(table_ref)
    adjoint = backward(pair(returned), rear, rear_waves, updates, half, table, False)
    backward(adjoint, front, front_waves, updates, 0, table, True)

    @pl.when(upper)
    def _():
        for turn in range(group):
            parts[turn][...] = updates[slot(me, kind, turn)]

    @pl.when(jnp.logical_not(upper))
    def _():
        for turn in range(group):
            parts[turn][...] = theirs[turn][...]


def place_kernel(owners, offsets, own, *rest):
    arrived, (near, middle, far, slab) = rest[:group], rest[group:]
    slab[...] = jnp.zeros_like(slab)
    odd = (arrived[1][...] + arrived[3][...]) + (arrived[5][...] + arrived[7][...])
    even = (arrived[2][...] + arrived[4][...]) + arrived[6][...]
    even = even + jnp.where(is_upper(), own[...], arrived[0][...])
    odd_position = 1 - (lax.axis_index("depth") & 1)
    for at, update in ((odd_position, odd), (1 - odd_position, even)):
        rows = pl.ds(start_of(at, owners, offsets), side)
        slab[:, rows, :] = slab[:, rows, :] + update
    middle[...] = slab[:, tile : 2 * tile]
    even_scan = (lax.axis_index("scan") & 1) == 0

    @pl.when(even_scan)
    def _():
        far[...] = slab[:, :tile]
        near[...] = slab[:, 2 * tile :]

    @pl.when(jnp.logical_not(even_scan))
    def _():
        near[...] = slab[:, :tile]
        far[...] = slab[:, 2 * tile :]


def last_kernel(block, middle, near, far, out):
    out[0] = block[...] - step_size * (middle[...] + near[...] + far[...])


def shards(object_slices, probe_wave, intensities, offsets, owners):
    scans = lax.axis_size("scan")
    depths = lax.axis_size("depth")
    axes = ("scan", "depth")
    step_table, fourier_table = tables()

    def call(kernel, out_shape, arguments, scratch=()):
        specs = [in_smem if a.dtype == jnp.int32 else in_vmem for a in arguments]
        return pl.pallas_call(
            kernel,
            out_shape=out_shape,
            in_specs=specs,
            out_specs=jax.tree.map(lambda _: in_vmem, out_shape),
            scratch_shapes=[pltpu.VMEM(shape, jnp.float32) for shape in scratch],
            compiler_params=params,
            name=kernel.__name__.removesuffix("_kernel"),
        )(*arguments)

    def at(scan, depth):
        return scan * depths + depth

    def ends(pairs):
        return [(b, a) for a, b in pairs]

    targets = [(i, first_target[i & 1] + q) for i in range(scans) for q in range(2)]
    gathers = []
    for turn in range(group):
        pairs = []
        for i, target in targets:
            source = target ^ rounds[i & 1][turn]
            if turn:
                pairs.append((at(i, source), at(i, target)))
            pairs.append((at(i, group + source), at(i ^ 1, target)))
        gathers.append(pairs)
    across = [(at(i, target), at(i ^ 1, target)) for i, target in targets]
    on_chip = [(i, i ^ 1) for i in range(scans)]
    next_chip = [(i, i + 1) for i in range(1, scans - 1, 2)]
    next_chip = next_chip + ends(next_chip)

    block = object_slices[0]
    far = lax.ppermute(block, "scan", next_chip)
    near = lax.ppermute(block, "scan", on_chip)
    measured = lax.ppermute(intensities, axes, across)
    far, near, measured = lax.optimization_barrier((far, near, measured))

    odd_window, even_window = call(
        cut_kernel,
        [window_type] * 2,
        (owners, offsets, block, near, far),
        [(2, 3 * tile, side)],
    )
    come = [
        lax.ppermute(odd_window if turn & 1 else even_window, axes, gathers[turn])
        for turn in (1, 2, 3, 4, 5, 6, 7, 0)
    ]
    late = come.pop()
    wave, front_waves, front = call(
        upper_kernel,
        [window_type, stack_type, stack_type],
        (probe_wave, even_window, late, *come[:4], step_table),
    )
    wave, rear_waves, rear = call(
        second_kernel,
        [window_type, stack_type, stack_type],
        (wave, even_window, late, *come[3:], step_table),
    )
    entering = lax.ppermute(wave, axes, across)
    full_stack = (group, 2, side, side)
    adjoint, *lower_parts = call(
        middle_kernel,
        [window_type] * (1 + group),
        (entering, front, rear, measured, step_table, fourier_table),
        [full_stack] * 2,
    )
    returned = lax.ppermute(adjoint, axes, ends(across))
    first_back = lax.ppermute(lower_parts[0], axes, ends(gathers[0]))
    parts = call(
        lower_kernel,
        [window_type] * group,
        (returned, front, front_waves, rear, rear_waves, step_table, *lower_parts),
        [full_stack],
    )
    landed = [first_back] + [
        lax.ppermute(parts[turn], axes, ends(gathers[turn])) for turn in range(1, group)
    ]
    near, middle, far = call(
        place_kernel,
        [tile_type] * 3,
        (owners, offsets, parts[0], *landed),
        [(2, 3 * tile, side)],
    )
    far = lax.ppermute(far, "scan", next_chip)
    near = lax.ppermute(near, "scan", on_chip)
    return call(
        last_kernel,
        jax.ShapeDtypeStruct(object_slices.shape, jnp.float32),
        (block, middle, near, far),
    )


def solution(mesh):
    return jax.shard_map(
        shards,
        mesh=mesh,
        in_specs=(P("depth", None, "scan", None), P(), P("scan", None, None), P("scan"), P("scan")),
        out_specs=P("depth", None, "scan", None),
        check_vma=False,
    )
```

```python
import functools

import jax
import jax.numpy as jnp
import numpy as np
from jax import lax
from jax.experimental import pallas as pl
from jax.experimental.pallas import tpu as pltpu
from jax.sharding import PartitionSpec as P

step_size = 0.25
side = 128
tile = 256
group = 4
long_cost = pl.CostEstimate(flops=2 * 10**10, bytes_accessed=2**25, transcendentals=0)
params = pltpu.CompilerParams(vmem_limit_bytes=48 * 2**20)
in_vmem = pl.BlockSpec(memory_space=pltpu.VMEM)
in_smem = pl.BlockSpec(memory_space=pltpu.SMEM)
window_type = jax.ShapeDtypeStruct((2, side, side), jnp.float32)
tile_type = jax.ShapeDtypeStruct((2, tile, side), jnp.float32)
slab_type = jax.ShapeDtypeStruct((2, 3 * tile, side), jnp.float32)
stack_type = jax.ShapeDtypeStruct((group, 2, side, side), jnp.float32)


def tables():
    index = np.arange(side)
    angles = 2.0 * np.pi * (index[:, None] * index[None, :] % side) / side
    fourier = (np.cos(angles) - 1j * np.sin(angles)) / np.sqrt(side)
    frequency = np.where(index < side // 2, index, index - side).astype(np.float64)
    phase = np.exp(-1j * np.pi / side * frequency * frequency)
    step = np.conj(fourier) @ (phase[:, None] * fourier)
    return [np.stack([m.real, m.imag]).astype(np.float32) for m in (step, fourier)]


def split(x):
    high = x.astype(jnp.bfloat16)
    return high, (x - high.astype(jnp.float32)).astype(jnp.bfloat16)


def dot(a, b):
    return jnp.dot(a, b, preferred_element_type=jnp.float32)


def beside(*parts):
    return jnp.concatenate(parts, 1)


def above(*parts):
    return jnp.concatenate(parts, 0)


def blocks(ref):
    real, imag = split(ref[0]), split(ref[1])
    left = [above(beside(r, -i), beside(i, r)) for r, i in zip(real, imag)]
    right = [above(beside(r, i), beside(-i, r)) for r, i in zip(real, imag)]
    return left, right


def two_sided(wave, table):
    (left_high, left_low), (right_high, right_low) = table
    high, low = split(above(*wave))
    both = dot(left_high, beside(high, low))
    left = both[:, :side] + both[:, side:] + dot(left_low, high)
    high, low = split(beside(left[:side], left[side:]))
    done = dot(high, right_high) + (dot(low, right_high) + dot(high, right_low))
    return done[:, :side], done[:, side:]


def times(a, b):
    return a[0] * b[0] - a[1] * b[1], a[0] * b[1] + a[1] * b[0]


def pair(ref, *at):
    return ref[(*at, 0)], ref[(*at, 1)]


def put(ref, value, *at):
    ref[(*at, 0)] = value[0]
    ref[(*at, 1)] = value[1]


def role():
    depth, scan = lax.axis_index("depth"), lax.axis_index("scan")
    row, column = depth // group, depth % group
    home = (column // 2) == (scan & 1)
    first, last = row == 0, row == group - 1
    return jnp.where(first, jnp.where(home, 0, 1), jnp.where(last, jnp.where(home, 3, 2), -1))


def column():
    return lax.axis_index("depth") % group


def start_of(at, owners, offsets):
    start = (owners[at] - lax.axis_index("scan") + 1) * tile + offsets[at]
    return jnp.clip(start, 0, 2 * tile)


def stage_kernel(block, top, bottom):
    top[...] = block[:, :side]
    bottom[...] = block[:, side:]


def by_scan_parity(even, odd):
    even_scan = (lax.axis_index("scan") & 1) == 0
    pl.when(even_scan)(even)
    pl.when(jnp.logical_not(even_scan))(odd)


def cut_kernel(owners, offsets, block, near_top, near_bottom, far, odd_out, even_out, slab):
    slab[:, tile : 2 * tile] = block[0]

    def even():
        slab[:, :tile] = far[...]
        slab[:, 2 * tile : 2 * tile + side] = near_top[...]

    def odd():
        slab[:, :side] = near_top[...]
        slab[:, side:tile] = near_bottom[...]
        slab[:, 2 * tile :] = far[...]

    by_scan_parity(even, odd)
    odd_position = 1 - (lax.axis_index("depth") & 1)
    for at, out in ((odd_position, odd_out), (1 - odd_position, even_out)):
        out[...] = slab[:, pl.ds(start_of(at, owners, offsets), side), :]


def collect(arrived, windows):
    me = column()
    for turn in range(group):
        windows[me ^ turn] = arrived[turn][...]


def forward_kernel(mine, wave_in, zero, one, two, three, table_ref, *rest):
    wave_out, waves, windows = rest[-3:]

    @pl.when(role() == mine)
    def _():
        collect((zero, one, two, three), windows)
        table = blocks(table_ref)
        wave = pair(wave_in)
        for layer in range(group):
            put(waves, wave, layer)
            wave = two_sided(times(wave, pair(windows, layer)), table)
        put(wave_out, wave)


def backward(adjoint, waves, windows, updates, table, last):
    for layer in reversed(range(group)):
        real, imag = times(pair(waves, layer), adjoint)
        put(updates, (real, -imag), layer)
        if layer or not last:
            adjoint = two_sided(times(pair(windows, layer), adjoint), table)
    return adjoint


def share(updates, parts):
    me = column()
    for turn in range(group):
        parts[turn][...] = updates[me ^ turn]


def far_kernel(wave_in, zero, one, two, three, measured, table_ref, fourier_ref, *rest):
    adjoint_out, parts, (waves, windows, updates) = rest[0], rest[1 : 1 + group], rest[1 + group :]

    @pl.when(role() == group - 1)
    def _():
        collect((zero, one, two, three), windows)
        table, fourier = blocks(table_ref), blocks(fourier_ref)
        wave = pair(wave_in)
        for layer in range(group):
            put(waves, wave, layer)
            last = layer == group - 1
            wave = two_sided(times(wave, pair(windows, layer)), fourier if last else table)
        far_real, far_imag = wave
        residual = far_real * far_real + far_imag * far_imag - measured[column() & 1]
        adjoint = two_sided((residual * far_real, -(residual * far_imag)), fourier)
        put(adjoint_out, backward(adjoint, waves, windows, updates, table, False))
        share(updates, parts)


def backward_kernel(mine, adjoint_in, waves, windows, table_ref, *rest):
    adjoint_out, parts, updates = rest[group], rest[group + 1 : -1], rest[-1]

    @pl.when(role() == mine)
    def _():
        adjoint = backward(
            pair(adjoint_in), waves, windows, updates, blocks(table_ref), mine == 0
        )
        if mine:
            put(adjoint_out, adjoint)
        share(updates, parts)


def place_kernel(owners, offsets, own, zero, one, two, three, slab, far):
    slab[...] = jnp.zeros_like(slab)
    local = (role() == 0) | (role() == group - 1)
    odd = one[...] + three[...]
    even = two[...] + jnp.where(local, own[...], zero[...])
    odd_position = 1 - (lax.axis_index("depth") & 1)
    for at, update in ((odd_position, odd), (1 - odd_position, even)):
        rows = pl.ds(start_of(at, owners, offsets), side)
        slab[:, rows, :] = slab[:, rows, :] + update

    def even_scan():
        far[...] = slab[:, :tile]

    def odd_scan():
        far[...] = slab[:, 2 * tile :]

    by_scan_parity(even_scan, odd_scan)


def near_kernel(slab, near_top, near_bottom):
    def even_scan():
        near_top[...] = slab[:, 2 * tile : 2 * tile + side]

    def odd_scan():
        near_top[...] = slab[:, :side]
        near_bottom[...] = slab[:, side:tile]

    by_scan_parity(even_scan, odd_scan)


def last_kernel(block, slab, near_top, near_bottom, far, out):
    for half, near in enumerate((near_top, near_bottom)):
        rows = slice(half * side, (half + 1) * side)
        mine = slab[:, tile + half * side : tile + (half + 1) * side]
        out[0, :, rows] = block[0, :, rows] - step_size * (mine + near[...] + far[:, rows])


def shards(object_slices, probe_wave, intensities, offsets, owners):
    scans = lax.axis_size("scan")
    depths = lax.axis_size("depth")
    axes = ("scan", "depth")
    step_table, fourier_table = tables()
    bottom = depths - group

    def call(kernel, name, out_shape, arguments, scratch=(), aliases=(), cost=None):
        specs = [in_smem if a.dtype == jnp.int32 else in_vmem for a in arguments]
        return pl.pallas_call(
            kernel,
            out_shape=out_shape,
            in_specs=specs,
            out_specs=jax.tree.map(lambda _: in_vmem, out_shape),
            scratch_shapes=[pltpu.VMEM(kind.shape, jnp.float32) for kind in scratch],
            input_output_aliases=dict(aliases),
            compiler_params=params,
            cost_estimate=cost,
            name=name,
        )(*arguments)

    def at(scan, depth):
        return scan * depths + depth

    def ends(pairs):
        return [(b, a) for a, b in pairs]

    targets = [(i, 2 * (i & 1) + q) for i in range(scans) for q in range(2)]
    gathers = []
    for turn in range(group):
        pairs = []
        for i, x in targets:
            source = x ^ turn
            if turn:
                pairs.append((at(i, source), at(i, x)))
                pairs.append((at(i, bottom + source), at(i, bottom + x)))
            pairs.append((at(i, group + source), at(i ^ 1, x)))
            pairs.append((at(i, 2 * group + source), at(i ^ 1, bottom + x)))
        gathers.append(pairs)
    hops = [
        [(at(i, x), at(i ^ 1, x)) for i, x in targets],
        [(at(i ^ 1, x), at(i ^ 1, bottom + x)) for i, x in targets],
        [(at(i ^ 1, bottom + x), at(i, bottom + x)) for i, x in targets],
    ]
    on_chip = [(i, i ^ 1) for i in range(scans)]
    downward = [(i, i + 1) for i in range(0, scans, 2)]
    next_chip = [(i, i + 1) for i in range(1, scans - 1, 2)]
    next_chip = next_chip + ends(next_chip)

    far = lax.ppermute(object_slices[0], "scan", next_chip)
    near_top, near_bottom = call(
        stage_kernel, "stage", [window_type] * 2, (object_slices[0],), cost=long_cost
    )
    near_top = lax.ppermute(near_top, "scan", on_chip)
    near_bottom = lax.ppermute(near_bottom, "scan", downward)
    odd_window, even_window = call(
        cut_kernel,
        "cut",
        [window_type] * 2,
        (owners, offsets, object_slices, near_top, near_bottom, far),
        [slab_type],
    )
    come = [
        lax.ppermute(odd_window if turn & 1 else even_window, axes, gathers[turn])
        for turn in (1, 2, 3, 0)
    ]
    late = come.pop()

    wave, waves, windows = call(
        functools.partial(forward_kernel, 0),
        "first",
        [window_type, stack_type, stack_type],
        (probe_wave, even_window, *come, step_table),
    )
    for mine, name in ((1, "second"), (2, "third")):
        wave = lax.ppermute(wave, axes, hops[mine - 1])
        wave, waves, windows = call(
            functools.partial(forward_kernel, mine),
            name,
            [window_type, stack_type, stack_type],
            (wave, late, *come, step_table, waves, windows),
            aliases=((6, 1), (7, 2)),
        )
    wave = lax.ppermute(wave, axes, hops[2])
    adjoint, *parts = call(
        far_kernel,
        "far",
        [window_type] * (1 + group),
        (wave, even_window, *come, intensities, step_table, fourier_table),
        [stack_type] * 3,
    )
    first_back = None
    for mine, name in ((2, "back_third"), (1, "back_second"), (0, "back_first")):
        adjoint = lax.ppermute(adjoint, axes, ends(hops[mine]))
        if mine == 0:
            first_back = lax.ppermute(parts[0], axes, ends(gathers[0]))
        adjoint, *parts = call(
            functools.partial(backward_kernel, mine),
            name,
            [window_type] * (1 + group),
            (adjoint, waves, windows, step_table, *parts),
            [stack_type],
            aliases=[(4 + turn, 1 + turn) for turn in range(group)],
        )
    landed = [
        lax.ppermute(parts[turn], axes, ends(gathers[turn])) for turn in range(1, group)
    ]
    slab, far = call(
        place_kernel,
        "place",
        [slab_type, tile_type],
        (owners, offsets, parts[0], first_back, *landed),
    )
    far = lax.ppermute(far, "scan", next_chip)
    near_top, near_bottom = call(
        near_kernel, "near", [window_type] * 2, (slab,), cost=long_cost
    )
    near_top = lax.ppermute(near_top, "scan", on_chip)
    near_bottom = lax.ppermute(near_bottom, "scan", ends(downward))
    return call(
        last_kernel,
        "last",
        jax.ShapeDtypeStruct(object_slices.shape, jnp.float32),
        (object_slices, slab, near_top, near_bottom, far),
    )


def solution(mesh):
    return jax.shard_map(
        shards,
        mesh=mesh,
        in_specs=(P("depth", None, "scan", None), P(), P("scan", None, None), P("scan"), P("scan")),
        out_specs=P("depth", None, "scan", None),
        check_vma=False,
    )
```

```python
import functools

import jax
import jax.numpy as jnp
import numpy as np
from jax import lax
from jax.experimental import pallas as pl
from jax.experimental.pallas import tpu as pltpu
from jax.sharding import PartitionSpec as P

step_size = 0.25
side = 128
tile = 256
group = 4
masks = (0, 1, 3, 2)
long_cost = pl.CostEstimate(flops=2 * 10**10, bytes_accessed=2**25, transcendentals=0)
params = pltpu.CompilerParams(vmem_limit_bytes=48 * 2**20)
in_vmem = pl.BlockSpec(memory_space=pltpu.VMEM)
in_smem = pl.BlockSpec(memory_space=pltpu.SMEM)
window_type = jax.ShapeDtypeStruct((2, side, side), jnp.float32)
tile_type = jax.ShapeDtypeStruct((2, tile, side), jnp.float32)
slab_type = jax.ShapeDtypeStruct((2, 3 * tile, side), jnp.float32)
stack_type = jax.ShapeDtypeStruct((group, 2, side, side), jnp.float32)


def tables():
    index = np.arange(side)
    angles = 2.0 * np.pi * (index[:, None] * index[None, :] % side) / side
    fourier = (np.cos(angles) - 1j * np.sin(angles)) / np.sqrt(side)
    frequency = np.where(index < side // 2, index, index - side).astype(np.float64)
    phase = np.exp(-1j * np.pi / side * frequency * frequency)
    step = np.conj(fourier) @ (phase[:, None] * fourier)
    return [np.stack([m.real, m.imag]).astype(np.float32) for m in (step, fourier)]


def split(x):
    high = x.astype(jnp.bfloat16)
    return high, (x - high.astype(jnp.float32)).astype(jnp.bfloat16)


def dot(a, b):
    return jnp.dot(a, b, preferred_element_type=jnp.float32)


def beside(*parts):
    return jnp.concatenate(parts, 1)


def above(*parts):
    return jnp.concatenate(parts, 0)


def blocks(ref):
    real, imag = split(ref[0]), split(ref[1])
    left = [above(beside(r, -i), beside(i, r)) for r, i in zip(real, imag)]
    right = [above(beside(r, i), beside(-i, r)) for r, i in zip(real, imag)]
    return left, right


def two_sided(wave, table):
    (left_high, left_low), (right_high, right_low) = table
    high, low = split(above(*wave))
    both = dot(left_high, beside(high, low))
    left = both[:, :side] + both[:, side:] + dot(left_low, high)
    high, low = split(beside(left[:side], left[side:]))
    done = dot(high, right_high) + (dot(low, right_high) + dot(high, right_low))
    return done[:, :side], done[:, side:]


def times(a, b):
    return a[0] * b[0] - a[1] * b[1], a[0] * b[1] + a[1] * b[0]


def pair(ref, *at):
    return ref[(*at, 0)], ref[(*at, 1)]


def put(ref, value, *at):
    ref[(*at, 0)] = value[0]
    ref[(*at, 1)] = value[1]


def role():
    depth, scan = lax.axis_index("depth"), lax.axis_index("scan")
    row, column = depth // group, depth % group
    home = (column & 1) == (scan & 1)
    first, last = row == 0, row == group - 1
    return jnp.where(first, jnp.where(home, 0, 1), jnp.where(last, jnp.where(home, 3, 2), -1))


def column():
    return lax.axis_index("depth") % group


def upper_position():
    return 1 - column() // 2


def start_of(at, owners, offsets):
    start = (owners[at] - lax.axis_index("scan") + 1) * tile + offsets[at]
    return jnp.clip(start, 0, 2 * tile)


def stage_kernel(block, top, bottom):
    top[...] = block[:, :side]
    bottom[...] = block[:, side:]


def by_scan_parity(even, odd):
    even_scan = (lax.axis_index("scan") & 1) == 0
    pl.when(even_scan)(even)
    pl.when(jnp.logical_not(even_scan))(odd)


def cut_kernel(owners, offsets, block, near_top, near_bottom, far, lower_out, upper_out, slab):
    slab[:, tile : 2 * tile] = block[0]

    def even():
        slab[:, :tile] = far[...]
        slab[:, 2 * tile : 2 * tile + side] = near_top[...]

    def odd():
        slab[:, :side] = near_top[...]
        slab[:, side:tile] = near_bottom[...]
        slab[:, 2 * tile :] = far[...]

    by_scan_parity(even, odd)
    upper = upper_position()
    for at, out in ((upper, upper_out), (1 - upper, lower_out)):
        out[...] = slab[:, pl.ds(start_of(at, owners, offsets), side), :]


def collect(arrived, windows):
    me = column()
    for turn in range(group):
        windows[me ^ masks[turn]] = arrived[turn][...]


def forward_kernel(mine, wave_in, zero, one, two, three, table_ref, *rest):
    wave_out, waves, windows = rest[-3:]

    @pl.when(role() == mine)
    def _():
        collect((zero, one, two, three), windows)
        table = blocks(table_ref)
        wave = pair(wave_in)
        for layer in range(group):
            put(waves, wave, layer)
            wave = two_sided(times(wave, pair(windows, layer)), table)
        put(wave_out, wave)


def backward(adjoint, waves, windows, updates, table, last):
    for layer in reversed(range(group)):
        real, imag = times(pair(waves, layer), adjoint)
        put(updates, (real, -imag), layer)
        if layer or not last:
            adjoint = two_sided(times(pair(windows, layer), adjoint), table)
    return adjoint


def share(updates, parts):
    me = column()
    for turn in range(group):
        parts[turn][...] = updates[me ^ masks[turn]]


def far_kernel(wave_in, zero, one, two, three, measured, table_ref, fourier_ref, *rest):
    adjoint_out, parts, (waves, windows, updates) = rest[0], rest[1 : 1 + group], rest[1 + group :]

    @pl.when(role() == group - 1)
    def _():
        collect((zero, one, two, three), windows)
        table, fourier = blocks(table_ref), blocks(fourier_ref)
        wave = pair(wave_in)
        for layer in range(group):
            put(waves, wave, layer)
            last = layer == group - 1
            wave = two_sided(times(wave, pair(windows, layer)), fourier if last else table)
        far_real, far_imag = wave
        residual = far_real * far_real + far_imag * far_imag - measured[column() // 2]
        adjoint = two_sided((residual * far_real, -(residual * far_imag)), fourier)
        put(adjoint_out, backward(adjoint, waves, windows, updates, table, False))
        share(updates, parts)


def backward_kernel(mine, adjoint_in, waves, windows, table_ref, *rest):
    parts, updates = rest[group : 2 * group], rest[-1]

    @pl.when(role() == mine)
    def _():
        adjoint = backward(
            pair(adjoint_in), waves, windows, updates, blocks(table_ref), mine == 0
        )
        if mine:
            put(rest[2 * group], adjoint)
        share(updates, parts)


def place_kernel(owners, offsets, own, zero, one, two, three, slab, far):
    slab[...] = jnp.zeros_like(slab)
    local = (role() == 0) | (role() == group - 1)
    late = two[...] + three[...]
    early = one[...] + jnp.where(local, own[...], zero[...])
    upper = upper_position()
    for at, update in ((upper, late), (1 - upper, early)):
        rows = pl.ds(start_of(at, owners, offsets), side)
        slab[:, rows, :] = slab[:, rows, :] + update

    def even_scan():
        far[...] = slab[:, :tile]

    def odd_scan():
        far[...] = slab[:, 2 * tile :]

    by_scan_parity(even_scan, odd_scan)


def near_kernel(slab, near_top, near_bottom):
    def even_scan():
        near_top[...] = slab[:, 2 * tile : 2 * tile + side]

    def odd_scan():
        near_top[...] = slab[:, :side]
        near_bottom[...] = slab[:, side:tile]

    by_scan_parity(even_scan, odd_scan)


def last_kernel(block, slab, near_top, near_bottom, far, out):
    for half, near in enumerate((near_top, near_bottom)):
        rows = slice(half * side, (half + 1) * side)
        mine = slab[:, tile + half * side : tile + (half + 1) * side]
        out[0, :, rows] = block[0, :, rows] - step_size * (mine + near[...] + far[:, rows])


def shards(object_slices, probe_wave, intensities, offsets, owners):
    scans = lax.axis_size("scan")
    depths = lax.axis_size("depth")
    axes = ("scan", "depth")
    step_table, fourier_table = tables()
    bottom = depths - group

    def call(kernel, name, out_shape, arguments, scratch=(), aliases=(), cost=None):
        specs = [in_smem if a.dtype == jnp.int32 else in_vmem for a in arguments]
        return pl.pallas_call(
            kernel,
            out_shape=out_shape,
            in_specs=specs,
            out_specs=jax.tree.map(lambda _: in_vmem, out_shape),
            scratch_shapes=[pltpu.VMEM(kind.shape, jnp.float32) for kind in scratch],
            input_output_aliases=dict(aliases),
            compiler_params=params,
            cost_estimate=cost,
            name=name,
        )(*arguments)

    def at(scan, depth):
        return scan * depths + depth

    def ends(pairs):
        return [(b, a) for a, b in pairs]

    targets = [(i, (i & 1) + 2 * q) for i in range(scans) for q in range(2)]
    gathers = []
    for turn in range(group):
        pairs = []
        for i, x in targets:
            source = x ^ masks[turn]
            if turn:
                pairs.append((at(i, source), at(i, x)))
                pairs.append((at(i, bottom + source), at(i, bottom + x)))
            pairs.append((at(i, group + source), at(i ^ 1, x)))
            pairs.append((at(i, 2 * group + source), at(i ^ 1, bottom + x)))
        gathers.append(pairs)
    hops = [
        [(at(i, x), at(i ^ 1, x)) for i, x in targets],
        [(at(i ^ 1, x), at(i ^ 1, bottom + x)) for i, x in targets],
        [(at(i ^ 1, bottom + x), at(i, bottom + x)) for i, x in targets],
    ]
    on_chip = [(i, i ^ 1) for i in range(scans)]
    downward = [(i, i + 1) for i in range(0, scans, 2)]
    next_chip = [(i, i + 1) for i in range(1, scans - 1, 2)]
    next_chip = next_chip + ends(next_chip)

    far = lax.ppermute(object_slices[0], "scan", next_chip)
    near_top, near_bottom = call(
        stage_kernel, "stage", [window_type] * 2, (object_slices[0],), cost=long_cost
    )
    near_top = lax.ppermute(near_top, "scan", on_chip)
    near_bottom = lax.ppermute(near_bottom, "scan", downward)
    lower_window, upper_window = call(
        cut_kernel,
        "cut",
        [window_type] * 2,
        (owners, offsets, object_slices, near_top, near_bottom, far),
        [slab_type],
    )
    come = [
        lax.ppermute(upper_window if turn & 2 else lower_window, axes, gathers[turn])
        for turn in range(group)
    ]
    late, *come = come

    wave, waves, windows = call(
        functools.partial(forward_kernel, 0),
        "first",
        [window_type, stack_type, stack_type],
        (probe_wave, lower_window, *come, step_table),
    )
    for mine, name in ((1, "second"), (2, "third")):
        wave = lax.ppermute(wave, axes, hops[mine - 1])
        wave, waves, windows = call(
            functools.partial(forward_kernel, mine),
            name,
            [window_type, stack_type, stack_type],
            (wave, late, *come, step_table, waves, windows),
            aliases=((6, 1), (7, 2)),
        )
    wave = lax.ppermute(wave, axes, hops[2])
    adjoint, *parts = call(
        far_kernel,
        "far",
        [window_type] * (1 + group),
        (wave, lower_window, *come, intensities, step_table, fourier_table),
        [stack_type] * 3,
    )
    for mine, name in ((2, "back_third"), (1, "back_second"), (0, "back_first")):
        adjoint = lax.ppermute(adjoint, axes, ends(hops[mine]))
        returned = call(
            functools.partial(backward_kernel, mine),
            name,
            [window_type] * (group + min(mine, 1)),
            (adjoint, waves, windows, step_table, *parts),
            [stack_type],
            aliases=[(4 + turn, turn) for turn in range(group)],
        )
        parts, adjoint = returned[:group], returned[-1]
    landed = [lax.ppermute(parts[turn], axes, ends(gathers[turn])) for turn in range(group)]
    slab, far = call(
        place_kernel,
        "place",
        [slab_type, tile_type],
        (owners, offsets, parts[0], *landed),
    )
    far = lax.ppermute(far, "scan", next_chip)
    near_top, near_bottom = call(
        near_kernel, "near", [window_type] * 2, (slab,), cost=long_cost
    )
    near_top = lax.ppermute(near_top, "scan", on_chip)
    near_bottom = lax.ppermute(near_bottom, "scan", ends(downward))
    return call(
        last_kernel,
        "last",
        jax.ShapeDtypeStruct(object_slices.shape, jnp.float32),
        (object_slices, slab, near_top, near_bottom, far),
    )


def solution(mesh):
    return jax.shard_map(
        shards,
        mesh=mesh,
        in_specs=(P("depth", None, "scan", None), P(), P("scan", None, None), P("scan"), P("scan")),
        out_specs=P("depth", None, "scan", None),
        check_vma=False,
    )
```

```python
import functools

import jax
import jax.numpy as jnp
import numpy as np
from jax import lax
from jax.experimental import pallas as pl
from jax.experimental.pallas import tpu as pltpu
from jax.sharding import PartitionSpec as P

step_size = 0.25
side = 128
tile = 256
group = 4
masks = (0, 2, 1, 3)
params = pltpu.CompilerParams(vmem_limit_bytes=48 * 2**20)
in_vmem = pl.BlockSpec(memory_space=pltpu.VMEM)
in_smem = pl.BlockSpec(memory_space=pltpu.SMEM)
window_type = jax.ShapeDtypeStruct((2, side, side), jnp.float32)
tile_type = jax.ShapeDtypeStruct((2, tile, side), jnp.float32)
slab_type = jax.ShapeDtypeStruct((2, 3 * tile, side), jnp.float32)
stack_type = jax.ShapeDtypeStruct((group, 2, side, side), jnp.float32)


def tables():
    index = np.arange(side)
    angles = 2.0 * np.pi * (index[:, None] * index[None, :] % side) / side
    fourier = (np.cos(angles) - 1j * np.sin(angles)) / np.sqrt(side)
    frequency = np.where(index < side // 2, index, index - side).astype(np.float64)
    phase = np.exp(-1j * np.pi / side * frequency * frequency)
    step = np.conj(fourier) @ (phase[:, None] * fourier)
    return [np.stack([m.real, m.imag]).astype(np.float32) for m in (step, fourier)]


def split(x):
    high = x.astype(jnp.bfloat16)
    return high, (x - high.astype(jnp.float32)).astype(jnp.bfloat16)


def dot(a, b):
    return jnp.dot(a, b, preferred_element_type=jnp.float32)


def beside(*parts):
    return jnp.concatenate(parts, 1)


def above(*parts):
    return jnp.concatenate(parts, 0)


def blocks(ref):
    real, imag = split(ref[0]), split(ref[1])
    left = [above(beside(r, -i), beside(i, r)) for r, i in zip(real, imag)]
    right = [above(beside(r, i), beside(-i, r)) for r, i in zip(real, imag)]
    return left, right


def two_sided(wave, table):
    (left_high, left_low), (right_high, right_low) = table
    high, low = split(above(*wave))
    both = dot(left_high, beside(high, low))
    left = both[:, :side] + both[:, side:] + dot(left_low, high)
    high, low = split(beside(left[:side], left[side:]))
    done = dot(high, right_high) + (dot(low, right_high) + dot(high, right_low))
    return done[:, :side], done[:, side:]


def times(a, b):
    return a[0] * b[0] - a[1] * b[1], a[0] * b[1] + a[1] * b[0]


def pair(ref, *at):
    return ref[(*at, 0)], ref[(*at, 1)]


def put(ref, value, *at):
    ref[(*at, 0)] = value[0]
    ref[(*at, 1)] = value[1]


def role():
    depth, scan = lax.axis_index("depth"), lax.axis_index("scan")
    row, home = depth // group, (depth % group) // 2 == (scan & 1)
    second, third = row == 1, row == 2
    return jnp.where(second, jnp.where(home, 0, 1), jnp.where(third, jnp.where(home, 3, 2), -1))


def column():
    return lax.axis_index("depth") % group


def upper_position():
    return 1 - (column() & 1)


def start_of(at, owners, offsets):
    start = (owners[at] - lax.axis_index("scan") + 1) * tile + offsets[at]
    return jnp.clip(start, 0, 2 * tile)


def by_scan_parity(even, odd):
    even_scan = (lax.axis_index("scan") & 1) == 0
    pl.when(even_scan)(even)
    pl.when(jnp.logical_not(even_scan))(odd)


def lay_kernel(far, block, slab):
    slab[:, tile : 2 * tile] = block[0]

    def even():
        slab[:, :tile] = far[...]

    def odd():
        slab[:, 2 * tile :] = far[...]

    by_scan_parity(even, odd)


def cut_kernel(near, owners, offsets, laid, lower_out, upper_out, slab):
    def even():
        slab[:, 2 * tile :] = near[...]

    def odd():
        slab[:, :tile] = near[...]

    by_scan_parity(even, odd)
    upper = upper_position()
    for at, out in ((upper, upper_out), (1 - upper, lower_out)):
        out[...] = slab[:, pl.ds(start_of(at, owners, offsets), side), :]


def collect(arrived, windows):
    me = column()
    for turn in range(group):
        windows[me ^ masks[turn]] = arrived[turn][...]


def forward_kernel(mine, wave_in, zero, one, two, three, table_ref, *rest):
    wave_out, waves, windows = rest[-3:]

    @pl.when(role() == mine)
    def _():
        collect((zero, one, two, three), windows)
        table = blocks(table_ref)
        wave = pair(wave_in)
        for layer in range(group):
            put(waves, wave, layer)
            wave = two_sided(times(wave, pair(windows, layer)), table)
        put(wave_out, wave)


def backward(adjoint, waves, windows, updates, table, last):
    for layer in reversed(range(group)):
        real, imag = times(pair(waves, layer), adjoint)
        put(updates, (real, -imag), layer)
        if layer or not last:
            adjoint = two_sided(times(pair(windows, layer), adjoint), table)
    return adjoint


def share(updates, parts):
    me = column()
    for turn in range(group):
        parts[turn][...] = updates[me ^ masks[turn]]


def far_kernel(wave_in, zero, one, two, three, measured, table_ref, fourier_ref, *rest):
    adjoint_out, parts, (waves, windows, updates) = rest[0], rest[1 : 1 + group], rest[1 + group :]

    @pl.when(role() == group - 1)
    def _():
        collect((zero, one, two, three), windows)
        table, fourier = blocks(table_ref), blocks(fourier_ref)
        wave = pair(wave_in)
        for layer in range(group):
            put(waves, wave, layer)
            last = layer == group - 1
            wave = two_sided(times(wave, pair(windows, layer)), fourier if last else table)
        far_real, far_imag = wave
        residual = far_real * far_real + far_imag * far_imag - measured[column() & 1]
        adjoint = two_sided((residual * far_real, -(residual * far_imag)), fourier)
        put(adjoint_out, backward(adjoint, waves, windows, updates, table, False))
        share(updates, parts)


def backward_kernel(mine, adjoint_in, waves, windows, table_ref, *rest):
    parts, updates = rest[group : 2 * group], rest[-1]

    @pl.when(role() == mine)
    def _():
        adjoint = backward(
            pair(adjoint_in), waves, windows, updates, blocks(table_ref), mine == 0
        )
        if mine:
            put(rest[2 * group], adjoint)
        share(updates, parts)


def place_kernel(owners, offsets, zero, one, two, three, slab, near, far):
    slab[...] = jnp.zeros_like(slab)
    upper = upper_position()
    for at, update in ((upper, two[...] + three[...]), (1 - upper, zero[...] + one[...])):
        rows = pl.ds(start_of(at, owners, offsets), side)
        slab[:, rows, :] = slab[:, rows, :] + update

    def even():
        far[...] = slab[:, :tile]
        near[...] = slab[:, 2 * tile :]

    def odd():
        near[...] = slab[:, :tile]
        far[...] = slab[:, 2 * tile :]

    by_scan_parity(even, odd)


def step_kernel(far, block, slab, out):
    out[...] = block[0] - step_size * (slab[:, tile : 2 * tile] + far[...])


def last_kernel(near, stepped, out):
    out[0] = stepped[...] - step_size * near[...]


def shards(object_slices, probe_wave, intensities, offsets, owners):
    scans = lax.axis_size("scan")
    depths = lax.axis_size("depth")
    axes = ("scan", "depth")
    step_table, fourier_table = tables()

    def call(kernel, name, out_shape, arguments, scratch=(), aliases=()):
        specs = [in_smem if a.dtype == jnp.int32 else in_vmem for a in arguments]
        return pl.pallas_call(
            kernel,
            out_shape=out_shape,
            in_specs=specs,
            out_specs=jax.tree.map(lambda _: in_vmem, out_shape),
            scratch_shapes=[pltpu.VMEM(kind.shape, jnp.float32) for kind in scratch],
            input_output_aliases=dict(aliases),
            compiler_params=params,
            name=name,
        )(*arguments)

    def at(scan, depth):
        return scan * depths + depth

    def ends(pairs):
        return [(b, a) for a, b in pairs]

    targets = [(i, 2 * (i & 1) + q) for i in range(scans) for q in range(2)]
    homes = [
        [(i, group + x), (i ^ 1, group + x), (i ^ 1, 2 * group + x), (i, 2 * group + x)]
        for i, x in targets
    ]
    gathers = [
        [
            (at(i, row * group + (x ^ mask)), at(*home[row]))
            for (i, x), home in zip(targets, homes)
            for row in range(group)
        ]
        for mask in masks
    ]
    hops = [
        [(at(*home[row]), at(*home[row + 1])) for home in homes] for row in range(group - 1)
    ]
    on_chip = [(i, i ^ 1) for i in range(scans)]
    next_chip = [(i, i + 1) for i in range(1, scans - 1, 2)]
    next_chip = next_chip + ends(next_chip)

    near = lax.ppermute(object_slices[0], "scan", on_chip)
    far = lax.ppermute(object_slices[0], "scan", next_chip)
    slab = call(lay_kernel, "lay", slab_type, (far, object_slices))
    lower_window, upper_window, slab = call(
        cut_kernel,
        "cut",
        [window_type, window_type, slab_type],
        (near, owners, offsets, slab),
        aliases=[(3, 2)],
    )
    come = [
        lax.ppermute(upper_window if turn & 2 else lower_window, axes, gathers[turn])
        for turn in range(group)
    ]

    wave, waves, windows = call(
        functools.partial(forward_kernel, 0),
        "first",
        [window_type, stack_type, stack_type],
        (probe_wave, *come, step_table),
    )
    for mine, name in ((1, "second"), (2, "third")):
        wave = lax.ppermute(wave, axes, hops[mine - 1])
        wave, waves, windows = call(
            functools.partial(forward_kernel, mine),
            name,
            [window_type, stack_type, stack_type],
            (wave, *come, step_table, waves, windows),
            aliases=((6, 1), (7, 2)),
        )
    wave = lax.ppermute(wave, axes, hops[2])
    adjoint, *parts = call(
        far_kernel,
        "far",
        [window_type] * (1 + group),
        (wave, *come, intensities, step_table, fourier_table),
        [stack_type] * 3,
    )
    for mine, name in ((2, "back_third"), (1, "back_second"), (0, "back_first")):
        adjoint = lax.ppermute(adjoint, axes, ends(hops[mine]))
        returned = call(
            functools.partial(backward_kernel, mine),
            name,
            [window_type] * (group + min(mine, 1)),
            (adjoint, waves, windows, step_table, *parts),
            [stack_type],
            aliases=[(4 + turn, turn) for turn in range(group)],
        )
        parts, adjoint = returned[:group], returned[-1]
    landed = [lax.ppermute(parts[turn], axes, ends(gathers[turn])) for turn in range(group)]
    slab, near, far = call(
        place_kernel,
        "place",
        [slab_type, tile_type, tile_type],
        (owners, offsets, *landed),
    )
    near = lax.ppermute(near, "scan", on_chip)
    far = lax.ppermute(far, "scan", next_chip)
    stepped = call(step_kernel, "step", tile_type, (far, object_slices, slab))
    return call(
        last_kernel,
        "last",
        jax.ShapeDtypeStruct(object_slices.shape, jnp.float32),
        (near, stepped),
    )


def solution(mesh):
    return jax.shard_map(
        shards,
        mesh=mesh,
        in_specs=(P("depth", None, "scan", None), P(), P("scan", None, None), P("scan"), P("scan")),
        out_specs=P("depth", None, "scan", None),
        check_vma=False,
    )
```

```python
import functools

import jax
import jax.numpy as jnp
import numpy as np
from jax import lax
from jax.experimental import pallas as pl
from jax.experimental.pallas import tpu as pltpu
from jax.sharding import PartitionSpec as P

step_size = 0.25
side = 128
tile = 256
group = 4
masks = (0, 2, 1, 3)
params = pltpu.CompilerParams(vmem_limit_bytes=48 * 2**20)
in_vmem = pl.BlockSpec(memory_space=pltpu.VMEM)
in_smem = pl.BlockSpec(memory_space=pltpu.SMEM)
window_type = jax.ShapeDtypeStruct((2, side, side), jnp.float32)
tile_type = jax.ShapeDtypeStruct((2, tile, side), jnp.float32)
slab_type = jax.ShapeDtypeStruct((2, 3 * tile, side), jnp.float32)
stack_type = jax.ShapeDtypeStruct((group, 2, side, side), jnp.float32)


def tables():
    index = np.arange(side)
    angles = 2.0 * np.pi * (index[:, None] * index[None, :] % side) / side
    fourier = (np.cos(angles) - 1j * np.sin(angles)) / np.sqrt(side)
    frequency = np.where(index < side // 2, index, index - side).astype(np.float64)
    phase = np.exp(-1j * np.pi / side * frequency * frequency)
    step = np.conj(fourier) @ (phase[:, None] * fourier)
    return [np.stack([m.real, m.imag]).astype(np.float32) for m in (step, fourier)]


def split(x):
    high = x.astype(jnp.bfloat16)
    return high, (x - high.astype(jnp.float32)).astype(jnp.bfloat16)


def dot(a, b):
    return jnp.dot(a, b, preferred_element_type=jnp.float32)


def beside(*parts):
    return jnp.concatenate(parts, 1)


def above(*parts):
    return jnp.concatenate(parts, 0)


def blocks(ref):
    real, imag = split(ref[0]), split(ref[1])
    left = [above(beside(r, -i), beside(i, r)) for r, i in zip(real, imag)]
    right = [above(beside(r, i), beside(-i, r)) for r, i in zip(real, imag)]
    return left, right


def two_sided(wave, table):
    (left_high, left_low), (right_high, right_low) = table
    high, low = split(above(*wave))
    both = dot(left_high, beside(high, low))
    left = both[:, :side] + both[:, side:] + dot(left_low, high)
    high, low = split(beside(left[:side], left[side:]))
    done = dot(high, right_high) + (dot(low, right_high) + dot(high, right_low))
    return done[:, :side], done[:, side:]


def times(a, b):
    return a[0] * b[0] - a[1] * b[1], a[0] * b[1] + a[1] * b[0]


def pair(ref, *at):
    return ref[(*at, 0)], ref[(*at, 1)]


def put(ref, value, *at):
    ref[(*at, 0)] = value[0]
    ref[(*at, 1)] = value[1]


def role():
    depth, scan = lax.axis_index("depth"), lax.axis_index("scan")
    row, home = depth // group, (depth % group) // 2 == (scan & 1)
    second, third = row == 1, row == 2
    return jnp.where(second, jnp.where(home, 0, 1), jnp.where(third, jnp.where(home, 3, 2), -1))


def column():
    return lax.axis_index("depth") % group


def upper_position():
    return 1 - (column() & 1)


def start_of(at, owners, offsets):
    start = (owners[at] - lax.axis_index("scan") + 1) * tile + offsets[at]
    return jnp.clip(start, 0, 2 * tile)


def by_scan_parity(even, odd):
    even_scan = (lax.axis_index("scan") & 1) == 0
    pl.when(even_scan)(even)
    pl.when(jnp.logical_not(even_scan))(odd)


def lay_kernel(far, block, slab):
    slab[:, tile : 2 * tile] = block[0]

    def even():
        slab[:, :tile] = far[...]

    def odd():
        slab[:, 2 * tile :] = far[...]

    by_scan_parity(even, odd)


def cut_kernel(near, owners, offsets, laid, lower_out, upper_out, slab):
    def even():
        slab[:, 2 * tile :] = near[...]

    def odd():
        slab[:, :tile] = near[...]

    by_scan_parity(even, odd)
    upper = upper_position()
    for at, out in ((upper, upper_out), (1 - upper, lower_out)):
        out[...] = slab[:, pl.ds(start_of(at, owners, offsets), side), :]


def collect(arrived, windows):
    me = column()
    for turn in range(group):
        windows[me ^ masks[turn]] = arrived[turn][...]


def forward_kernel(mine, wave_in, zero, one, two, three, table_ref, *rest):
    wave_out, waves, windows = rest[-3:]

    @pl.when(role() == mine)
    def _():
        collect((zero, one, two, three), windows)
        table = blocks(table_ref)
        wave = pair(wave_in)
        for layer in range(group):
            put(waves, wave, layer)
            wave = two_sided(times(wave, pair(windows, layer)), table)
        put(wave_out, wave)


def backward(adjoint, waves, windows, updates, table, last):
    for layer in reversed(range(group)):
        real, imag = times(pair(waves, layer), adjoint)
        put(updates, (real, -imag), layer)
        if layer or not last:
            adjoint = two_sided(times(pair(windows, layer), adjoint), table)
    return adjoint


def share(updates, parts):
    me = column()
    for turn in range(group):
        parts[turn][...] = updates[me ^ masks[turn]]


def far_kernel(wave_in, zero, one, two, three, measured, table_ref, fourier_ref, *rest):
    adjoint_out, parts, (waves, windows, updates) = rest[0], rest[1 : 1 + group], rest[1 + group :]

    @pl.when(role() == group - 1)
    def _():
        collect((zero, one, two, three), windows)
        table, fourier = blocks(table_ref), blocks(fourier_ref)
        wave = pair(wave_in)
        for layer in range(group):
            put(waves, wave, layer)
            last = layer == group - 1
            wave = two_sided(times(wave, pair(windows, layer)), fourier if last else table)
        far_real, far_imag = wave
        residual = far_real * far_real + far_imag * far_imag - measured[column() & 1]
        adjoint = two_sided((residual * far_real, -(residual * far_imag)), fourier)
        put(adjoint_out, backward(adjoint, waves, windows, updates, table, False))
        share(updates, parts)


def backward_kernel(mine, adjoint_in, waves, windows, table_ref, *rest):
    rest, updates = rest[group if mine else 0 : -1], rest[-1]

    @pl.when(role() == mine)
    def _():
        adjoint = backward(
            pair(adjoint_in), waves, windows, updates, blocks(table_ref), mine == 0
        )
        if mine:
            put(rest[group], adjoint)
        share(updates, rest[:group])


def place_kernel(owners, offsets, *rest):
    landed, (slab, near, far) = rest[: 2 * group], rest[2 * group :]
    slab[...] = jnp.zeros_like(slab)
    zero, one, two, three = [landed[r][...] + landed[group + r][...] for r in range(group)]
    upper = upper_position()
    for at, update in ((upper, two + three), (1 - upper, zero + one)):
        rows = pl.ds(start_of(at, owners, offsets), side)
        slab[:, rows, :] = slab[:, rows, :] + update

    def even():
        far[...] = slab[:, :tile]
        near[...] = slab[:, 2 * tile :]

    def odd():
        near[...] = slab[:, :tile]
        far[...] = slab[:, 2 * tile :]

    by_scan_parity(even, odd)


def step_kernel(far, block, slab, out):
    out[...] = block[0] - step_size * (slab[:, tile : 2 * tile] + far[...])


def last_kernel(near, stepped, out):
    out[0] = stepped[...] - step_size * near[...]


def shards(object_slices, probe_wave, intensities, offsets, owners):
    scans = lax.axis_size("scan")
    depths = lax.axis_size("depth")
    axes = ("scan", "depth")
    step_table, fourier_table = tables()

    def call(kernel, name, out_shape, arguments, scratch=(), aliases=()):
        specs = [in_smem if a.dtype == jnp.int32 else in_vmem for a in arguments]
        return pl.pallas_call(
            kernel,
            out_shape=out_shape,
            in_specs=specs,
            out_specs=jax.tree.map(lambda _: in_vmem, out_shape),
            scratch_shapes=[pltpu.VMEM(kind.shape, jnp.float32) for kind in scratch],
            input_output_aliases=dict(aliases),
            compiler_params=params,
            name=name,
        )(*arguments)

    def at(scan, depth):
        return scan * depths + depth

    def ends(pairs):
        return [(b, a) for a, b in pairs]

    targets = [(i, 2 * (i & 1) + q) for i in range(scans) for q in range(2)]
    homes = [
        [(i, group + x), (i ^ 1, group + x), (i ^ 1, 2 * group + x), (i, 2 * group + x)]
        for i, x in targets
    ]
    gathers = [
        [
            [
                (at(i, row * group + (x ^ mask)), at(*home[row]))
                for (i, x), home in zip(targets, homes)
                for row in rows
            ]
            for mask in masks
        ]
        for rows in ((0,), range(1, group))
    ]
    hops = [
        [(at(*home[row]), at(*home[row + 1])) for home in homes] for row in range(group - 1)
    ]
    on_chip = [(i, i ^ 1) for i in range(scans)]
    next_chip = [(i, i + 1) for i in range(1, scans - 1, 2)]
    next_chip = next_chip + ends(next_chip)

    near = lax.ppermute(object_slices[0], "scan", on_chip)
    far = lax.ppermute(object_slices[0], "scan", next_chip)
    slab = call(lay_kernel, "lay", slab_type, (far, object_slices))
    lower_window, upper_window, slab = call(
        cut_kernel,
        "cut",
        [window_type, window_type, slab_type],
        (near, owners, offsets, slab),
        aliases=[(3, 2)],
    )
    come_first, come = [
        [
            lax.ppermute(upper_window if turn & 2 else lower_window, axes, pairs[turn])
            for turn in range(group)
        ]
        for pairs in gathers
    ]

    wave, waves, windows = call(
        functools.partial(forward_kernel, 0),
        "first",
        [window_type, stack_type, stack_type],
        (probe_wave, *come_first, step_table),
    )
    for mine, name in ((1, "second"), (2, "third")):
        wave = lax.ppermute(wave, axes, hops[mine - 1])
        wave, waves, windows = call(
            functools.partial(forward_kernel, mine),
            name,
            [window_type, stack_type, stack_type],
            (wave, *come, step_table, waves, windows),
            aliases=((6, 1), (7, 2)),
        )
    wave = lax.ppermute(wave, axes, hops[2])
    adjoint, *parts = call(
        far_kernel,
        "far",
        [window_type] * (1 + group),
        (wave, *come, intensities, step_table, fourier_table),
        [stack_type] * 3,
    )
    for mine, name in ((2, "back_third"), (1, "back_second")):
        adjoint = lax.ppermute(adjoint, axes, ends(hops[mine]))
        *parts, adjoint = call(
            functools.partial(backward_kernel, mine),
            name,
            [window_type] * (group + 1),
            (adjoint, waves, windows, step_table, *parts),
            [stack_type],
            aliases=[(4 + turn, turn) for turn in range(group)],
        )
    adjoint = lax.ppermute(adjoint, axes, ends(hops[0]))
    landed = [lax.ppermute(parts[turn], axes, ends(gathers[1][turn])) for turn in range(group)]
    parts = call(
        functools.partial(backward_kernel, 0),
        "back_first",
        [window_type] * group,
        (adjoint, waves, windows, step_table),
        [stack_type],
    )
    landed += [lax.ppermute(parts[turn], axes, ends(gathers[0][turn])) for turn in range(group)]
    slab, near, far = call(
        place_kernel,
        "place",
        [slab_type, tile_type, tile_type],
        (owners, offsets, *landed),
    )
    near = lax.ppermute(near, "scan", on_chip)
    far = lax.ppermute(far, "scan", next_chip)
    stepped = call(step_kernel, "step", tile_type, (far, object_slices, slab))
    return call(
        last_kernel,
        "last",
        jax.ShapeDtypeStruct(object_slices.shape, jnp.float32),
        (near, stepped),
    )


def solution(mesh):
    return jax.shard_map(
        shards,
        mesh=mesh,
        in_specs=(P("depth", None, "scan", None), P(), P("scan", None, None), P("scan"), P("scan")),
        out_specs=P("depth", None, "scan", None),
        check_vma=False,
    )
```

```python
import functools

import jax
import jax.numpy as jnp
import numpy as np
from jax import lax
from jax.experimental import pallas as pl
from jax.experimental.pallas import tpu as pltpu
from jax.sharding import PartitionSpec as P

step_size = 0.25
side = 128
tile = 256
group = 4
masks = (0, 2, 1, 3)
back_masks = (1, 2, 3, 0)
params = pltpu.CompilerParams(vmem_limit_bytes=48 * 2**20)
in_vmem = pl.BlockSpec(memory_space=pltpu.VMEM)
in_smem = pl.BlockSpec(memory_space=pltpu.SMEM)
window_type = jax.ShapeDtypeStruct((2, side, side), jnp.float32)
tile_type = jax.ShapeDtypeStruct((2, tile, side), jnp.float32)
slab_type = jax.ShapeDtypeStruct((2, 3 * tile, side), jnp.float32)
stack_type = jax.ShapeDtypeStruct((group, 2, side, side), jnp.float32)


def tables():
    index = np.arange(side)
    angles = 2.0 * np.pi * (index[:, None] * index[None, :] % side) / side
    fourier = (np.cos(angles) - 1j * np.sin(angles)) / np.sqrt(side)
    frequency = np.where(index < side // 2, index, index - side).astype(np.float64)
    phase = np.exp(-1j * np.pi / side * frequency * frequency)
    step = np.conj(fourier) @ (phase[:, None] * fourier)
    return [np.stack([m.real, m.imag]).astype(np.float32) for m in (step, fourier)]


def split(x):
    high = x.astype(jnp.bfloat16)
    return high, (x - high.astype(jnp.float32)).astype(jnp.bfloat16)


def dot(a, b):
    return jnp.dot(a, b, preferred_element_type=jnp.float32)


def beside(*parts):
    return jnp.concatenate(parts, 1)


def above(*parts):
    return jnp.concatenate(parts, 0)


def blocks(ref):
    real, imag = split(ref[0]), split(ref[1])
    left = [above(beside(r, -i), beside(i, r)) for r, i in zip(real, imag)]
    right = [above(beside(r, i), beside(-i, r)) for r, i in zip(real, imag)]
    return left, right


def two_sided(wave, table):
    (left_high, left_low), (right_high, right_low) = table
    high, low = split(above(*wave))
    both = dot(left_high, beside(high, low))
    left = both[:, :side] + both[:, side:] + dot(left_low, high)
    high, low = split(beside(left[:side], left[side:]))
    done = dot(high, right_high) + (dot(low, right_high) + dot(high, right_low))
    return done[:, :side], done[:, side:]


def times(a, b):
    return a[0] * b[0] - a[1] * b[1], a[0] * b[1] + a[1] * b[0]


def pair(ref, *at):
    return ref[(*at, 0)], ref[(*at, 1)]


def put(ref, value, *at):
    ref[(*at, 0)] = value[0]
    ref[(*at, 1)] = value[1]


def role():
    depth, scan = lax.axis_index("depth"), lax.axis_index("scan")
    row, home = depth // group, (depth % group) // 2 == (scan & 1)
    top, bottom = row == 0, row == group - 1
    return jnp.where(top, jnp.where(home, 0, 1), jnp.where(bottom, jnp.where(home, 3, 2), -1))


def column():
    return lax.axis_index("depth") % group


def upper_position():
    return 1 - (column() & 1)


def start_of(at, owners, offsets):
    start = (owners[at] - lax.axis_index("scan") + 1) * tile + offsets[at]
    return jnp.clip(start, 0, 2 * tile)


def by_scan_parity(even, odd):
    even_scan = (lax.axis_index("scan") & 1) == 0
    pl.when(even_scan)(even)
    pl.when(jnp.logical_not(even_scan))(odd)


def stage_kernel(block, slab):
    slab[:, tile : 2 * tile] = block[0]


def lay_kernel(far, staged, slab):
    def even():
        slab[:, :tile] = far[...]

    def odd():
        slab[:, 2 * tile :] = far[...]

    by_scan_parity(even, odd)


def cut_kernel(near, owners, offsets, laid, lower_out, upper_out, own, slab):
    def even():
        slab[:, 2 * tile :] = near[...]

    def odd():
        slab[:, :tile] = near[...]

    by_scan_parity(even, odd)
    upper = upper_position()
    for at, out in ((upper, upper_out), (1 - upper, lower_out)):
        out[...] = slab[:, pl.ds(start_of(at, owners, offsets), side), :]
    own[...] = lower_out[...]


def collect(arrived, windows):
    me = column()
    for turn in range(group):
        windows[me ^ masks[turn]] = arrived[turn][...]


def forward_kernel(mine, wave_in, zero, one, two, three, table_ref, *rest):
    wave_out, waves, windows = rest[-3:]

    @pl.when(role() == mine)
    def _():
        collect((zero, one, two, three), windows)
        table = blocks(table_ref)
        wave = pair(wave_in)
        for layer in range(group):
            put(waves, wave, layer)
            wave = two_sided(times(wave, pair(windows, layer)), table)
        put(wave_out, wave)


def backward(adjoint, waves, windows, updates, table, last):
    for layer in reversed(range(group)):
        real, imag = times(pair(waves, layer), adjoint)
        put(updates, (real, -imag), layer)
        if layer or not last:
            adjoint = two_sided(times(pair(windows, layer), adjoint), table)
    return adjoint


def share(updates, parts):
    me = column()
    for turn in range(group):
        parts[turn][...] = updates[me ^ back_masks[turn]]


def far_kernel(wave_in, zero, one, two, three, measured, table_ref, fourier_ref, *rest):
    adjoint_out, parts, (waves, windows, updates) = rest[0], rest[1 : 1 + group], rest[1 + group :]

    @pl.when(role() == group - 1)
    def _():
        collect((zero, one, two, three), windows)
        table, fourier = blocks(table_ref), blocks(fourier_ref)
        wave = pair(wave_in)
        for layer in range(group):
            put(waves, wave, layer)
            last = layer == group - 1
            wave = two_sided(times(wave, pair(windows, layer)), fourier if last else table)
        far_real, far_imag = wave
        residual = far_real * far_real + far_imag * far_imag - measured[column() & 1]
        adjoint = two_sided((residual * far_real, -(residual * far_imag)), fourier)
        put(adjoint_out, backward(adjoint, waves, windows, updates, table, False))
        share(updates, parts)


def backward_kernel(mine, adjoint_in, waves, windows, table_ref, *rest):
    rest, updates = rest[group:-1], rest[-1]

    @pl.when(role() == mine)
    def _():
        adjoint = backward(
            pair(adjoint_in), waves, windows, updates, blocks(table_ref), mine == 0
        )
        if mine:
            put(rest[group], adjoint)
        share(updates, rest[:group])


def place_kernel(owners, offsets, own, one, two, three, zero, slab, near, far):
    slab[...] = jnp.zeros_like(slab)
    local = (role() == 0) | (role() == group - 1)
    late = one[...] + three[...]
    early = two[...] + jnp.where(local, own[...], zero[...])
    upper = upper_position()
    for at, update in ((upper, late), (1 - upper, early)):
        rows = pl.ds(start_of(at, owners, offsets), side)
        slab[:, rows, :] = slab[:, rows, :] + update

    def even():
        far[...] = slab[:, :tile]
        near[...] = slab[:, 2 * tile :]

    def odd():
        near[...] = slab[:, :tile]
        far[...] = slab[:, 2 * tile :]

    by_scan_parity(even, odd)


def step_kernel(far, block, slab, out):
    out[...] = block[0] - step_size * (slab[:, tile : 2 * tile] + far[...])


def last_kernel(near, stepped, out):
    out[0] = stepped[...] - step_size * near[...]


def shards(object_slices, probe_wave, intensities, offsets, owners):
    scans = lax.axis_size("scan")
    depths = lax.axis_size("depth")
    axes = ("scan", "depth")
    step_table, fourier_table = tables()

    def call(kernel, name, out_shape, arguments, scratch=(), aliases=()):
        specs = [in_smem if a.dtype == jnp.int32 else in_vmem for a in arguments]
        return pl.pallas_call(
            kernel,
            out_shape=out_shape,
            in_specs=specs,
            out_specs=jax.tree.map(lambda _: in_vmem, out_shape),
            scratch_shapes=[pltpu.VMEM(kind.shape, jnp.float32) for kind in scratch],
            input_output_aliases=dict(aliases),
            compiler_params=params,
            name=name,
        )(*arguments)

    def at(scan, depth):
        return scan * depths + depth

    def ends(pairs):
        return [(b, a) for a, b in pairs]

    targets = [(i, 2 * (i & 1) + q) for i in range(scans) for q in range(2)]
    bottom = depths - group
    homes = [[(i, x), (i ^ 1, x), (i ^ 1, bottom + x), (i, bottom + x)] for i, x in targets]

    def sends(mask):
        pairs = [
            (at(i, row * group + (x ^ mask)), at(*home[row]))
            for (i, x), home in zip(targets, homes)
            for row in range(group)
        ]
        return [(a, b) for a, b in pairs if a != b]

    hops = [
        [(at(*home[row]), at(*home[row + 1])) for home in homes] for row in range(group - 1)
    ]
    on_chip = [(i, i ^ 1) for i in range(scans)]
    next_chip = [(i, i + 1) for i in range(1, scans - 1, 2)]
    next_chip = next_chip + ends(next_chip)

    near = lax.ppermute(object_slices[0], "scan", on_chip)
    far = lax.ppermute(object_slices[0], "scan", next_chip)
    slab = call(stage_kernel, "stage", slab_type, (object_slices,))
    slab = call(lay_kernel, "lay", slab_type, (far, slab), aliases=[(1, 0)])
    lower_window, upper_window, own, slab = call(
        cut_kernel,
        "cut",
        [window_type] * 3 + [slab_type],
        (near, owners, offsets, slab),
        aliases=[(3, 3)],
    )
    come = [
        lax.ppermute(upper_window if mask & 1 else lower_window, axes, sends(mask))
        for mask in masks
    ]

    wave, waves, windows = call(
        functools.partial(forward_kernel, 0),
        "first",
        [window_type, stack_type, stack_type],
        (probe_wave, own, *come[1:], step_table),
    )
    for mine, name in ((1, "second"), (2, "third")):
        wave = lax.ppermute(wave, axes, hops[mine - 1])
        wave, waves, windows = call(
            functools.partial(forward_kernel, mine),
            name,
            [window_type, stack_type, stack_type],
            (wave, *come, step_table, waves, windows),
            aliases=((6, 1), (7, 2)),
        )
    wave = lax.ppermute(wave, axes, hops[2])
    adjoint, *parts = call(
        far_kernel,
        "far",
        [window_type] * (1 + group),
        (wave, own, *come[1:], intensities, step_table, fourier_table),
        [stack_type] * 3,
    )
    for mine, name in ((2, "back_third"), (1, "back_second"), (0, "back_first")):
        adjoint = lax.ppermute(adjoint, axes, ends(hops[mine]))
        returned = call(
            functools.partial(backward_kernel, mine),
            name,
            [window_type] * (group + min(mine, 1)),
            (adjoint, waves, windows, step_table, *parts),
            [stack_type],
            aliases=[(4 + turn, turn) for turn in range(group)],
        )
        parts, adjoint = returned[:group], returned[-1]
    landed = [
        lax.ppermute(part, axes, ends(sends(mask))) for mask, part in zip(back_masks, parts)
    ]
    slab, near, far = call(
        place_kernel,
        "place",
        [slab_type, tile_type, tile_type],
        (owners, offsets, parts[-1], *landed),
    )
    near = lax.ppermute(near, "scan", on_chip)
    far = lax.ppermute(far, "scan", next_chip)
    stepped = call(step_kernel, "step", tile_type, (far, object_slices, slab))
    return call(
        last_kernel,
        "last",
        jax.ShapeDtypeStruct(object_slices.shape, jnp.float32),
        (near, stepped),
    )


def solution(mesh):
    return jax.shard_map(
        shards,
        mesh=mesh,
        in_specs=(P("depth", None, "scan", None), P(), P("scan", None, None), P("scan"), P("scan")),
        out_specs=P("depth", None, "scan", None),
        check_vma=False,
    )
```

```python
import functools

import jax
import jax.numpy as jnp
import numpy as np
from jax import lax
from jax.experimental import pallas as pl
from jax.experimental.pallas import tpu as pltpu
from jax.sharding import PartitionSpec as P

step_size = 0.25
side = 128
tile = 256
group = 4
params = pltpu.CompilerParams(vmem_limit_bytes=48 * 2**20)
in_vmem = pl.BlockSpec(memory_space=pltpu.VMEM)
in_smem = pl.BlockSpec(memory_space=pltpu.SMEM)
window_type = jax.ShapeDtypeStruct((2, side, side), jnp.float32)
tile_type = jax.ShapeDtypeStruct((2, tile, side), jnp.float32)
slab_type = jax.ShapeDtypeStruct((2, 3 * tile, side), jnp.float32)
double_type = jax.ShapeDtypeStruct((2 * group, 2, side, side), jnp.float32)
stack_type = jax.ShapeDtypeStruct((group, 2, side, side), jnp.float32)


def tables():
    index = np.arange(side)
    angles = 2.0 * np.pi * (index[:, None] * index[None, :] % side) / side
    fourier = (np.cos(angles) - 1j * np.sin(angles)) / np.sqrt(side)
    frequency = np.where(index < side // 2, index, index - side).astype(np.float64)
    phase = np.exp(-1j * np.pi / side * frequency * frequency)
    step = np.conj(fourier) @ (phase[:, None] * fourier)
    return [np.stack([m.real, m.imag]).astype(np.float32) for m in (step, fourier)]


def split(x):
    high = x.astype(jnp.bfloat16)
    return high, (x - high.astype(jnp.float32)).astype(jnp.bfloat16)


def dot(a, b):
    return jnp.dot(a, b, preferred_element_type=jnp.float32)


def beside(*parts):
    return jnp.concatenate(parts, 1)


def above(*parts):
    return jnp.concatenate(parts, 0)


def blocks(ref):
    real, imag = split(ref[0]), split(ref[1])
    left = [above(beside(r, -i), beside(i, r)) for r, i in zip(real, imag)]
    right = [above(beside(r, i), beside(-i, r)) for r, i in zip(real, imag)]
    return left, right


def two_sided(wave, table):
    (left_high, left_low), (right_high, right_low) = table
    high, low = split(above(*wave))
    both = dot(left_high, beside(high, low))
    left = both[:, :side] + both[:, side:] + dot(left_low, high)
    high, low = split(beside(left[:side], left[side:]))
    done = dot(high, right_high) + (dot(low, right_high) + dot(high, right_low))
    return done[:, :side], done[:, side:]


def times(a, b):
    return a[0] * b[0] - a[1] * b[1], a[0] * b[1] + a[1] * b[0]


def pair(ref, *at):
    return ref[(*at, 0)], ref[(*at, 1)]


def put(ref, value, *at):
    ref[(*at, 0)] = value[0]
    ref[(*at, 1)] = value[1]


def role():
    depth, scan = lax.axis_index("depth"), lax.axis_index("scan")
    row, home = depth // group, (depth % group) // 2 == (scan & 1)
    top, bottom = row == 0, row == group - 1
    return jnp.where(top, jnp.where(home, 0, 1), jnp.where(bottom & home, 2, -1))


def column():
    return lax.axis_index("depth") % group


def upper_position():
    return 1 - (column() & 1)


def start_of(at, owners, offsets):
    start = (owners[at] - lax.axis_index("scan") + 1) * tile + offsets[at]
    return jnp.clip(start, 0, 2 * tile)


def by_scan_parity(even, odd):
    even_scan = (lax.axis_index("scan") & 1) == 0
    pl.when(even_scan)(even)
    pl.when(jnp.logical_not(even_scan))(odd)


def stage_kernel(block, slab):
    slab[:, tile : 2 * tile] = block[0]


def lay_kernel(far, staged, slab):
    def even():
        slab[:, :tile] = far[...]

    def odd():
        slab[:, 2 * tile :] = far[...]

    by_scan_parity(even, odd)


def cut_kernel(near, owners, offsets, laid, lower_out, upper_out, own, slab):
    def even():
        slab[:, 2 * tile :] = near[...]

    def odd():
        slab[:, :tile] = near[...]

    by_scan_parity(even, odd)
    upper = upper_position()
    for at, out in ((upper, upper_out), (1 - upper, lower_out)):
        out[...] = slab[:, pl.ds(start_of(at, owners, offsets), side), :]
    own[...] = lower_out[...]


def collect(arrived, windows, base=0):
    me = column()
    for mask, window in enumerate(arrived):
        windows[base + (me ^ mask)] = window[...]


def forward_kernel(mine, wave_in, zero, one, two, three, table_ref, *rest):
    wave_out, waves, windows = rest[-3:]

    @pl.when(role() == mine)
    def _():
        collect((zero, one, two, three), windows)
        table = blocks(table_ref)
        wave = pair(wave_in)
        for layer in range(group):
            put(waves, wave, layer)
            wave = two_sided(times(wave, pair(windows, layer)), table)
        put(wave_out, wave)


def backward(adjoint, waves, windows, updates, table, last):
    for layer in reversed(range(updates.shape[0])):
        real, imag = times(pair(waves, layer), adjoint)
        put(updates, (real, -imag), layer)
        if layer or not last:
            adjoint = two_sided(times(pair(windows, layer), adjoint), table)
    return adjoint


def share(updates, parts, base=0):
    me = column()
    for mask, part in enumerate(parts):
        part[...] = updates[base + (me ^ mask)]


def far_kernel(wave_in, *rest):
    third, fourth, (measured, table_ref, fourier_ref), rest = (
        rest[:group],
        rest[group : 2 * group],
        rest[2 * group : 2 * group + 3],
        rest[2 * group + 3 :],
    )
    adjoint_out, third_parts, fourth_parts = rest[0], rest[1 : 1 + group], rest[1 + group : -3]
    waves, windows, updates = rest[-3:]

    @pl.when(role() == 2)
    def _():
        collect(third, windows)
        collect(fourth, windows, group)
        table, fourier = blocks(table_ref), blocks(fourier_ref)
        wave = pair(wave_in)
        for layer in range(2 * group):
            put(waves, wave, layer)
            last = layer == 2 * group - 1
            wave = two_sided(times(wave, pair(windows, layer)), fourier if last else table)
        far_real, far_imag = wave
        residual = far_real * far_real + far_imag * far_imag - measured[column() & 1]
        adjoint = two_sided((residual * far_real, -(residual * far_imag)), fourier)
        put(adjoint_out, backward(adjoint, waves, windows, updates, table, False))
        share(updates, third_parts)
        share(updates, fourth_parts, group)


def backward_kernel(mine, extra, adjoint_in, waves, windows, table_ref, *rest):
    rest, updates = rest[group + extra : -1], rest[-1]

    @pl.when(role() == mine)
    def _():
        adjoint = backward(
            pair(adjoint_in), waves, windows, updates, blocks(table_ref), mine == 0
        )
        if mine:
            put(rest[group], adjoint)
        share(updates, rest[:group])


def place_kernel(owners, offsets, first_own, fourth_own, *rest):
    (zero, one, two, three), fourth, (slab, near, far) = rest[:group], rest[group:-3], rest[-3:]
    slab[...] = jnp.zeros_like(slab)
    mine = role()
    own = jnp.where(mine == 0, first_own[...], jnp.where(mine == 2, fourth_own[...], zero[...]))
    late = (one[...] + three[...]) + (fourth[0][...] + fourth[2][...])
    early = (two[...] + fourth[1][...]) + own
    upper = upper_position()
    for at, update in ((upper, late), (1 - upper, early)):
        rows = pl.ds(start_of(at, owners, offsets), side)
        slab[:, rows, :] = slab[:, rows, :] + update

    def even():
        far[...] = slab[:, :tile]
        near[...] = slab[:, 2 * tile :]

    def odd():
        near[...] = slab[:, :tile]
        far[...] = slab[:, 2 * tile :]

    by_scan_parity(even, odd)


def step_kernel(far, block, slab, out):
    out[...] = block[0] - step_size * (slab[:, tile : 2 * tile] + far[...])


def last_kernel(near, stepped, out):
    out[0] = stepped[...] - step_size * near[...]


def shards(object_slices, probe_wave, intensities, offsets, owners):
    scans = lax.axis_size("scan")
    depths = lax.axis_size("depth")
    axes = ("scan", "depth")
    step_table, fourier_table = tables()

    def call(kernel, name, out_shape, arguments, scratch=(), aliases=(), after=()):
        specs = [in_smem if a.dtype == jnp.int32 else in_vmem for a in arguments]
        specs += [pl.BlockSpec(memory_space=pl.ANY)] * len(after)
        return pl.pallas_call(
            kernel,
            out_shape=out_shape,
            in_specs=specs,
            out_specs=jax.tree.map(lambda _: in_vmem, out_shape),
            scratch_shapes=[pltpu.VMEM(kind.shape, jnp.float32) for kind in scratch],
            input_output_aliases=dict(aliases),
            compiler_params=params,
            name=name,
        )(*arguments, *after)

    def at(scan, depth):
        return scan * depths + depth

    def ends(pairs):
        return [(b, a) for a, b in pairs]

    targets = [(i, 2 * (i & 1) + q) for i in range(scans) for q in range(2)]
    bottom = depths - group
    homes = [[(i, x), (i ^ 1, x), (i, bottom + x), (i, bottom + x)] for i, x in targets]

    def sends(mask, *groups):
        pairs = [
            (at(i, row * group + (x ^ mask)), at(*home[row]))
            for (i, x), home in zip(targets, homes)
            for row in groups
        ]
        return [(a, b) for a, b in pairs if a != b]

    hops = [[(at(*home[row]), at(*home[row + 1])) for home in homes] for row in range(2)]
    on_chip = [(i, i ^ 1) for i in range(scans)]
    next_chip = [(i, i + 1) for i in range(1, scans - 1, 2)]
    next_chip = next_chip + ends(next_chip)

    near = lax.ppermute(object_slices[0], "scan", on_chip)
    far = lax.ppermute(object_slices[0], "scan", next_chip)
    slab = call(stage_kernel, "stage", slab_type, (object_slices,))
    slab = call(lay_kernel, "lay", slab_type, (far, slab), aliases=[(1, 0)])
    lower_window, upper_window, own, slab = call(
        cut_kernel,
        "cut",
        [window_type] * 3 + [slab_type],
        (near, owners, offsets, slab),
        aliases=[(3, 3)],
    )
    def gather(mask, *groups):
        return lax.ppermute(upper_window if mask & 1 else lower_window, axes, sends(mask, *groups))

    two, three = gather(2, 0, 1, 2), gather(3, 0, 1, 2)
    mate = gather(1, 0, 3)
    zero, one = gather(0, 1, 2), gather(1, 1, 2)
    fourth_two, fourth_three = gather(2, 3), gather(3, 3)

    wave, waves, windows = call(
        functools.partial(forward_kernel, 0),
        "first",
        [window_type, stack_type, stack_type],
        (probe_wave, own, mate, two, three, step_table),
    )
    wave = lax.ppermute(wave, axes, hops[0])
    wave, waves, windows = call(
        functools.partial(forward_kernel, 1),
        "second",
        [window_type, stack_type, stack_type],
        (wave, zero, one, two, three, step_table, waves, windows),
        aliases=((6, 1), (7, 2)),
    )
    wave = lax.ppermute(wave, axes, hops[1])
    third, fourth = (zero, one, two, three), (own, mate, fourth_two, fourth_three)
    adjoint, *parts = call(
        far_kernel,
        "far",
        [window_type] * (1 + 2 * group),
        (wave, *third, *fourth, intensities, step_table, fourier_table),
        [double_type] * 3,
    )
    parts, (fourth_own, *fourth_parts) = parts[:group], parts[group:]

    def scatter(part, mask, *groups):
        return lax.ppermute(part, axes, ends(sends(mask, *groups)))

    for mine, name in ((1, "back_second"), (0, "back_first")):
        adjoint = lax.ppermute(adjoint, axes, ends(hops[mine]))
        early = ()
        if mine:
            landed = early = [scatter(part, 1 + turn, 3) for turn, part in enumerate(fourth_parts)]
        returned = call(
            functools.partial(backward_kernel, mine, len(early)),
            name,
            [window_type] * (group + mine),
            (adjoint, waves, windows, step_table, *parts),
            [stack_type],
            aliases=[(4 + mask, mask) for mask in range(group)],
            after=early,
        )
        parts, adjoint = returned[:group], returned[-1]
    landed = [
        scatter(part, mask, *((1, 2) if mask == 0 else (0, 1, 2)))
        for mask, part in enumerate(parts)
    ] + landed
    slab, near, far = call(
        place_kernel,
        "place",
        [slab_type, tile_type, tile_type],
        (owners, offsets, parts[0], fourth_own, *landed),
    )
    near = lax.ppermute(near, "scan", on_chip)
    far = lax.ppermute(far, "scan", next_chip)
    stepped = call(step_kernel, "step", tile_type, (far, object_slices, slab))
    return call(
        last_kernel,
        "last",
        jax.ShapeDtypeStruct(object_slices.shape, jnp.float32),
        (near, stepped),
    )


def solution(mesh):
    return jax.shard_map(
        shards,
        mesh=mesh,
        in_specs=(P("depth", None, "scan", None), P(), P("scan", None, None), P("scan"), P("scan")),
        out_specs=P("depth", None, "scan", None),
        check_vma=False,
    )
```

```python
import functools

import jax
import jax.numpy as jnp
import numpy as np
from jax import lax
from jax.experimental import pallas as pl
from jax.experimental.pallas import tpu as pltpu
from jax.sharding import PartitionSpec as P

step_size = 0.25
side = 128
tile = 256
group = 4
params = pltpu.CompilerParams(vmem_limit_bytes=48 * 2**20)
in_vmem = pl.BlockSpec(memory_space=pltpu.VMEM)
window_type = jax.ShapeDtypeStruct((2, side, side), jnp.float32)
tile_type = jax.ShapeDtypeStruct((2, tile, side), jnp.float32)
slab_type = jax.ShapeDtypeStruct((2, 3 * tile, side), jnp.float32)
double_type = jax.ShapeDtypeStruct((2 * group, 2, side, side), jnp.float32)
stack_type = jax.ShapeDtypeStruct((group, 2, side, side), jnp.float32)


def tables():
    index = np.arange(side)
    angles = 2.0 * np.pi * (index[:, None] * index[None, :] % side) / side
    fourier = (np.cos(angles) - 1j * np.sin(angles)) / np.sqrt(side)
    frequency = np.where(index < side // 2, index, index - side).astype(np.float64)
    phase = np.exp(-1j * np.pi / side * frequency * frequency)
    step = np.conj(fourier) @ (phase[:, None] * fourier)
    return [np.stack([m.real, m.imag]).astype(np.float32) for m in (step, fourier)]


def split(x):
    high = x.astype(jnp.bfloat16)
    return high, (x - high.astype(jnp.float32)).astype(jnp.bfloat16)


def dot(a, b):
    return jnp.dot(a, b, preferred_element_type=jnp.float32)


def beside(*parts):
    return jnp.concatenate(parts, 1)


def above(*parts):
    return jnp.concatenate(parts, 0)


def blocks(ref):
    real, imag = split(ref[0]), split(ref[1])
    left = [above(beside(r, -i), beside(i, r)) for r, i in zip(real, imag)]
    right = [above(beside(r, i), beside(-i, r)) for r, i in zip(real, imag)]
    return left, right


def two_sided(wave, table):
    (left_high, left_low), (right_high, right_low) = table
    high, low = split(above(*wave))
    both = dot(left_high, beside(high, low))
    left = both[:, :side] + both[:, side:] + dot(left_low, high)
    high, low = split(beside(left[:side], left[side:]))
    done = dot(high, right_high) + (dot(low, right_high) + dot(high, right_low))
    return done[:, :side], done[:, side:]


def times(a, b):
    return a[0] * b[0] - a[1] * b[1], a[0] * b[1] + a[1] * b[0]


def pair(ref, *at):
    return ref[(*at, 0)], ref[(*at, 1)]


def put(ref, value, *at):
    ref[(*at, 0)] = value[0]
    ref[(*at, 1)] = value[1]


def role():
    depth, scan = lax.axis_index("depth"), lax.axis_index("scan")
    row, home = depth // group, (depth % group) // 2 == (scan & 1)
    top, bottom = row == 0, row == group - 1
    return jnp.where(top, jnp.where(home, 0, 1), jnp.where(bottom & home, 2, -1))


def column():
    return lax.axis_index("depth") % group


def upper_position():
    return 1 - (column() & 1)


def start_of(at, starts):
    chosen = lax.broadcasted_iota(jnp.int32, starts.shape, 1) == at
    start = jnp.sum(jnp.where(chosen, starts[...], 0.0)).astype(jnp.int32)
    return jnp.clip(start, 0, 2 * tile)


def by_scan_parity(even, odd):
    even_scan = (lax.axis_index("scan") & 1) == 0
    pl.when(even_scan)(even)
    pl.when(jnp.logical_not(even_scan))(odd)


def stage_kernel(owners, offsets, block, starts, slab):
    tiles = owners[...] - (lax.axis_index("scan") - 1)
    starts[...] = (tiles * tile + offsets[...]).astype(jnp.float32)
    slab[:, tile : 2 * tile] = block[0]


def lay_kernel(far, staged, slab):
    def even():
        slab[:, :tile] = far[...]

    def odd():
        slab[:, 2 * tile :] = far[...]

    by_scan_parity(even, odd)


def cut_kernel(near, starts, laid, lower_out, upper_out, own, slab):
    def even():
        slab[:, 2 * tile :] = near[...]

    def odd():
        slab[:, :tile] = near[...]

    by_scan_parity(even, odd)
    upper = upper_position()
    for at, out in ((upper, upper_out), (1 - upper, lower_out)):
        out[...] = slab[:, pl.ds(start_of(at, starts), side), :]
    own[...] = lower_out[...]


def collect(arrived, windows, base=0):
    me = column()
    for mask, window in enumerate(arrived):
        windows[base + (me ^ mask)] = window[...]


def forward_kernel(mine, wave_in, zero, one, two, three, table_ref, *rest):
    wave_out, waves, windows = rest[-3:]

    @pl.when(role() == mine)
    def _():
        collect((zero, one, two, three), windows)
        table = blocks(table_ref)
        wave = pair(wave_in)
        for layer in range(group):
            put(waves, wave, layer)
            wave = two_sided(times(wave, pair(windows, layer)), table)
        put(wave_out, wave)


def backward(adjoint, waves, windows, updates, table, last):
    for layer in reversed(range(updates.shape[0])):
        real, imag = times(pair(waves, layer), adjoint)
        put(updates, (real, -imag), layer)
        if layer or not last:
            adjoint = two_sided(times(pair(windows, layer), adjoint), table)
    return adjoint


def share(updates, parts, base=0):
    me = column()
    for mask, part in enumerate(parts):
        part[...] = updates[base + (me ^ mask)]


def far_kernel(wave_in, *rest):
    third, fourth, (measured, table_ref, fourier_ref), rest = (
        rest[:group],
        rest[group : 2 * group],
        rest[2 * group : 2 * group + 3],
        rest[2 * group + 3 :],
    )
    adjoint_out, third_parts, fourth_parts = rest[0], rest[1 : 1 + group], rest[1 + group : -3]
    waves, windows, updates = rest[-3:]

    @pl.when(role() == 2)
    def _():
        collect(third, windows)
        collect(fourth, windows, group)
        table, fourier = blocks(table_ref), blocks(fourier_ref)
        wave = pair(wave_in)
        for layer in range(2 * group):
            put(waves, wave, layer)
            last = layer == 2 * group - 1
            wave = two_sided(times(wave, pair(windows, layer)), fourier if last else table)
        far_real, far_imag = wave
        residual = far_real * far_real + far_imag * far_imag - measured[column() & 1]
        adjoint = two_sided((residual * far_real, -(residual * far_imag)), fourier)
        put(adjoint_out, backward(adjoint, waves, windows, updates, table, False))
        share(updates, third_parts)
        share(updates, fourth_parts, group)


def backward_kernel(mine, extra, adjoint_in, waves, windows, table_ref, *rest):
    rest, updates = rest[group + extra : -1], rest[-1]

    @pl.when(role() == mine)
    def _():
        adjoint = backward(
            pair(adjoint_in), waves, windows, updates, blocks(table_ref), mine == 0
        )
        if mine:
            put(rest[group], adjoint)
        share(updates, rest[:group])


def place_kernel(starts, first_own, fourth_own, *rest):
    (zero, one, two, three), fourth, (slab, near, far) = rest[:group], rest[group:-3], rest[-3:]
    slab[...] = jnp.zeros_like(slab)
    mine = role()
    own = jnp.where(mine == 0, first_own[...], jnp.where(mine == 2, fourth_own[...], zero[...]))
    late = (one[...] + three[...]) + (fourth[0][...] + fourth[2][...])
    early = (two[...] + fourth[1][...]) + own
    upper = upper_position()
    for at, update in ((upper, late), (1 - upper, early)):
        rows = pl.ds(start_of(at, starts), side)
        slab[:, rows, :] = slab[:, rows, :] + update

    def even():
        far[...] = slab[:, :tile]
        near[...] = slab[:, 2 * tile :]

    def odd():
        near[...] = slab[:, :tile]
        far[...] = slab[:, 2 * tile :]

    by_scan_parity(even, odd)


def step_kernel(far, block, slab, out):
    out[...] = block[0] - step_size * (slab[:, tile : 2 * tile] + far[...])


def last_kernel(near, stepped, out):
    out[0] = stepped[...] - step_size * near[...]


def shards(object_slices, probe_wave, intensities, offsets, owners):
    scans = lax.axis_size("scan")
    depths = lax.axis_size("depth")
    axes = ("scan", "depth")
    step_table, fourier_table = tables()

    def call(kernel, name, out_shape, arguments, scratch=(), aliases=(), after=()):
        specs = [in_vmem] * len(arguments)
        specs += [pl.BlockSpec(memory_space=pl.ANY)] * len(after)
        return pl.pallas_call(
            kernel,
            out_shape=out_shape,
            in_specs=specs,
            out_specs=jax.tree.map(lambda _: in_vmem, out_shape),
            scratch_shapes=[pltpu.VMEM(kind.shape, jnp.float32) for kind in scratch],
            input_output_aliases=dict(aliases),
            compiler_params=params,
            name=name,
        )(*arguments, *after)

    def at(scan, depth):
        return scan * depths + depth

    def ends(pairs):
        return [(b, a) for a, b in pairs]

    targets = [(i, 2 * (i & 1) + q) for i in range(scans) for q in range(2)]
    bottom = depths - group
    homes = [[(i, x), (i ^ 1, x), (i, bottom + x), (i, bottom + x)] for i, x in targets]

    def sends(mask, *groups):
        pairs = [
            (at(i, row * group + (x ^ mask)), at(*home[row]))
            for (i, x), home in zip(targets, homes)
            for row in groups
        ]
        return [(a, b) for a, b in pairs if a != b]

    hops = [[(at(*home[row]), at(*home[row + 1])) for home in homes] for row in range(2)]
    on_chip = [(i, i ^ 1) for i in range(scans)]
    next_chip = [(i, i + 1) for i in range(1, scans - 1, 2)]
    next_chip = next_chip + ends(next_chip)

    near = lax.ppermute(object_slices[0], "scan", on_chip)
    far = lax.ppermute(object_slices[0], "scan", next_chip)
    starts_type = jax.ShapeDtypeStruct((1, offsets.shape[0]), jnp.float32)
    starts, slab = call(
        stage_kernel,
        "stage",
        [starts_type, slab_type],
        (owners[None], offsets[None], object_slices),
    )
    slab = call(lay_kernel, "lay", slab_type, (far, slab), aliases=[(1, 0)])
    lower_window, upper_window, own, slab = call(
        cut_kernel,
        "cut",
        [window_type] * 3 + [slab_type],
        (near, starts, slab),
        aliases=[(2, 3)],
    )
    def gather(mask, *groups):
        return lax.ppermute(upper_window if mask & 1 else lower_window, axes, sends(mask, *groups))

    two, three = gather(2, 0, 1, 2), gather(3, 0, 1, 2)
    mate = gather(1, 0, 3)
    zero, one = gather(0, 1, 2), gather(1, 1, 2)
    fourth_two, fourth_three = gather(2, 3), gather(3, 3)

    wave, waves, windows = call(
        functools.partial(forward_kernel, 0),
        "first",
        [window_type, stack_type, stack_type],
        (probe_wave, own, mate, two, three, step_table),
    )
    wave = lax.ppermute(wave, axes, hops[0])
    wave, waves, windows = call(
        functools.partial(forward_kernel, 1),
        "second",
        [window_type, stack_type, stack_type],
        (wave, zero, one, two, three, step_table, waves, windows),
        aliases=((6, 1), (7, 2)),
    )
    wave = lax.ppermute(wave, axes, hops[1])
    third, fourth = (zero, one, two, three), (own, mate, fourth_two, fourth_three)
    adjoint, *parts = call(
        far_kernel,
        "far",
        [window_type] * (1 + 2 * group),
        (wave, *third, *fourth, intensities, step_table, fourier_table),
        [double_type] * 3,
    )
    parts, (fourth_own, *fourth_parts) = parts[:group], parts[group:]

    def scatter(part, mask, *groups):
        return lax.ppermute(part, axes, ends(sends(mask, *groups)))

    for mine, name in ((1, "back_second"), (0, "back_first")):
        adjoint = lax.ppermute(adjoint, axes, ends(hops[mine]))
        early = ()
        if mine:
            landed = early = [scatter(part, 1 + turn, 3) for turn, part in enumerate(fourth_parts)]
        returned = call(
            functools.partial(backward_kernel, mine, len(early)),
            name,
            [window_type] * (group + mine),
            (adjoint, waves, windows, step_table, *parts),
            [stack_type],
            aliases=[(4 + mask, mask) for mask in range(group)],
            after=early,
        )
        parts, adjoint = returned[:group], returned[-1]
    landed = [
        scatter(part, mask, *((1, 2) if mask == 0 else (0, 1, 2)))
        for mask, part in enumerate(parts)
    ] + landed
    slab, near, far = call(
        place_kernel,
        "place",
        [slab_type, tile_type, tile_type],
        (starts, parts[0], fourth_own, *landed),
    )
    near = lax.ppermute(near, "scan", on_chip)
    far = lax.ppermute(far, "scan", next_chip)
    stepped = call(step_kernel, "step", tile_type, (far, object_slices, slab))
    return call(
        last_kernel,
        "last",
        jax.ShapeDtypeStruct(object_slices.shape, jnp.float32),
        (near, stepped),
    )


def solution(mesh):
    return jax.shard_map(
        shards,
        mesh=mesh,
        in_specs=(P("depth", None, "scan", None), P(), P("scan", None, None), P("scan"), P("scan")),
        out_specs=P("depth", None, "scan", None),
        check_vma=False,
    )
```
